32 devices in a mesh: src: 4 (over y, x), tgt: 8 (over z, core).
Axes of the slice: x: 2, y: 2, z: 4, core: 2. Of those that a mesh axis runs over, the one named last changes fastest.
Arguments:
- tile_cost: bfloat16 [384, 512, 512], P(('src', 'tgt')), may hold values from -2.5 to 7.5
- tile_pairs: int32 [384, 2], P(('src', 'tgt')), may hold values from 0 to 95, as said below
- tile_counts: int32 [32], P(('src', 'tgt')), may hold values from 3 to 12, as said below
- src_mass: float32 [12288], P('src'), may hold values from 0.25 to 4
- tgt_mass: float32 [49152], P('tgt'), may hold values from 0.25 to 4
- targets_t: bfloat16 [64, 49152], P(None, 'tgt'), may hold values from -18 to 18
Outputs:
- mapped_t: float32 [64, 12288], P(None, ('src', 'tgt'))
The draws below stay inside these ranges and needn't reach their ends.
Inputs may be any that keep to these rules, and one draw needn't show every extreme that they name: `tile_pairs`: device d of the src+tgt order owns slots d * 12 to (d + 1) * 12 - 1. Its first tile_counts[d] slots hold distinct kept pairs whose source tile lies among its src index's 6 tiles and whose target tile among its tgt index's 12 tiles; its other slots repeat its first slot. Every source tile is in exactly 8 kept pairs, every target tile in at least one. `tile_counts`: over the devices of one src index the counts sum to 48; some device of every src index holds 12; every device holds at least (8 * 6 - 12) // (8 - 1) - 2.
All inputs are finite; a program needn't handle non-finite values.
Results may differ from the reference program's by a relative error of at most 0.0029.
Values may be sent and summed in bfloat16 or wider, within the bound.
A program may use at most 64 MiB of HBM per device.

```python
import math
import jax
import jax.numpy as jnp
from jax import lax

TILE = 512
DIM = 64
LOAD = 6
TGT_TILES = 12
ITERS = 2
CAP = 12
SRC_TILES = 6
NS = 12288
NT = 49152
N_SRC = 4
N_TGT = 8


def tile_layout(key):
    base_key = jax.random.fold_in(key, 7)
    row_keys = jax.random.split(base_key, N_SRC)

    def one_row(row_key):
        order_key, move_key = jax.random.split(row_key)
        order = jax.random.permutation(order_key, N_TGT).astype(jnp.int32)
        remain = N_TGT * LOAD - CAP
        basic = remain // (N_TGT - 1)
        extra = remain % (N_TGT - 1)
        position = jnp.arange(N_TGT, dtype=jnp.int32)
        profile = jnp.where(position == 0, CAP, basic + (position - 1 < extra).astype(jnp.int32))
        moves = jax.random.randint(move_key, (N_TGT,), 0, 3).astype(jnp.int32)
        giving = jnp.where((position % 2 == 1) & (position + 1 < N_TGT), moves, 0)
        received = jnp.concatenate([jnp.zeros((1,), jnp.int32), giving[:-1]])
        profile = (profile - giving + received).astype(jnp.int32)
        return jnp.zeros((N_TGT,), jnp.int32).at[order].set(profile)
    counts = jax.vmap(one_row)(row_keys)
    row_start = jnp.cumsum(counts, axis=1) - counts
    col_start = jnp.cumsum(counts, axis=0) - counts
    slot_range = jnp.arange(CAP, dtype=jnp.int32)
    alive = slot_range[None, None, :] < counts[:, :, None]
    used = jnp.where(alive, slot_range[None, None, :], 0)
    src_local = (row_start[:, :, None] + used) % SRC_TILES
    tgt_local = (col_start[:, :, None] + used) % TGT_TILES
    src_block = jnp.arange(N_SRC, dtype=jnp.int32)[:, None, None] * SRC_TILES
    tgt_block = jnp.arange(N_TGT, dtype=jnp.int32)[None, :, None] * TGT_TILES
    pairs = jnp.stack([src_block + src_local, tgt_block + tgt_local], axis=-1).astype(jnp.int32)
    return (counts.reshape(-1), pairs.reshape(N_SRC * N_TGT * CAP, 2))


def draw_tile_pairs(key, part):
    return tile_layout(key)[1]


def draw_tile_counts(key, part):
    return tile_layout(key)[0]


def draw_tile_cost(key, part):
    first_key = jax.random.fold_in(jax.random.fold_in(key, 11), 0)
    shape = (N_SRC * N_TGT * CAP, TILE, TILE)
    return jax.random.uniform(first_key, shape, jnp.float32, 0.0, 4.0).astype(jnp.bfloat16)


def block_scale(key, extent, shards, smallest, high):
    def one(axis_at, shards_of):
        heights = jax.random.uniform(jax.random.fold_in(jax.random.fold_in(key, 6), axis_at), (shards_of,), jnp.float32, smallest / len(shards), high / len(shards))
        return jnp.repeat(jnp.exp(heights), extent[axis_at] // shards_of).reshape((-1,) + (1,) * (len(extent) - axis_at - 1))

    factor_of = one(*shards[0])
    for cut in shards[1:]:
        factor_of = factor_of * one(*cut)
    return factor_of


def centred(stream_key, shape, scale, most, shards=(), kind=jnp.bfloat16):
    drawn = scale * jax.random.normal(stream_key, shape, jnp.float32)
    if shards:
        drawn = drawn * block_scale(stream_key, shape, shards, -0.22, 0.18)
    return jnp.clip(drawn, -most, most).astype(kind)


def setup_inputs(seed: int = 0) -> dict:
    streams_of = jax.random.split(jax.random.key(seed), 7)
    tile_cost = draw_tile_cost(jax.random.fold_in(streams_of[6], 71), 0)
    tile_pairs = draw_tile_pairs(jax.random.fold_in(streams_of[6], 71), 0)
    tile_counts = draw_tile_counts(jax.random.fold_in(streams_of[6], 71), 0)
    src_mass = jnp.clip(jnp.exp(math.log(4.0) - 2.7725887 * jax.random.uniform(streams_of[3], (NS,), jnp.float32) ** block_scale(streams_of[3], (NS,), ((0, 4),), -0.2, 0.2)), 0.25, 4.0)
    tgt_mass = jnp.clip(jnp.exp(math.log(4.0) - 2.7725887 * jax.random.uniform(streams_of[4], (NT,), jnp.float32) ** block_scale(streams_of[4], (NT,), ((0, 8),), -0.2, 0.2)), 0.25, 4.0)
    targets_t = centred(streams_of[5], (DIM, NT), 3.0, 18.0, ((1, 8),))
    return {"tile_cost": tile_cost, "tile_pairs": tile_pairs, "tile_counts": tile_counts, "src_mass": src_mass, "tgt_mass": tgt_mass, "targets_t": targets_t}


entropic = 0.02
negative_floor = -1e30


def fold_pair(first, second):
    larger = jnp.maximum(first[0], second[0])
    return (larger, first[1] * jnp.exp(first[0] - larger) + second[1] * jnp.exp(second[0] - larger))


def merge_into(totals, position, part):
    before = (lax.dynamic_index_in_dim(totals[0], position, 0, False), lax.dynamic_index_in_dim(totals[1], position, 0, False))
    after = fold_pair(before, part)
    return (lax.dynamic_update_index_in_dim(totals[0], after[0], position, 0), lax.dynamic_update_index_in_dim(totals[1], after[1], position, 0))


def potential(merged, masses):
    return entropic * jnp.log(masses) - entropic * (merged[0] + jnp.log(merged[1])).reshape(-1)


def reference(tile_cost, tile_pairs, tile_counts, src_mass, tgt_mass, targets_t):
    slot_total = tile_cost.shape[0]
    edge = tile_cost.shape[1]
    slot_ids = jnp.arange(slot_total, dtype=jnp.int32)
    alive = (slot_ids % CAP) < jnp.repeat(tile_counts, CAP, total_repeat_length=slot_total)
    src_tiles = src_mass.shape[0] // edge
    tgt_tiles = tgt_mass.shape[0] // edge

    def empty_pair(count):
        return (jnp.full((count, edge), negative_floor, jnp.float32), jnp.zeros((count, edge), jnp.float32))

    def row_sweep(tgt_pot):
        def advance(totals, slot_index):
            cost_tile = tile_cost[slot_index].astype(jnp.float32)
            src_tile = tile_pairs[slot_index, 0].astype(jnp.int32)
            tgt_tile = tile_pairs[slot_index, 1].astype(jnp.int32)
            column_pot = lax.dynamic_slice_in_dim(tgt_pot, tgt_tile * edge, edge)
            scores = (column_pot[None, :] - cost_tile) / entropic
            maxima = jnp.max(scores, axis=1)
            sums = jnp.sum(jnp.exp(scores - maxima[:, None]), axis=1)
            maxima = jnp.where(alive[slot_index], maxima, negative_floor)
            sums = jnp.where(alive[slot_index], sums, 0.0)
            return merge_into(totals, src_tile, (maxima, sums)), None
        result, unused = lax.scan(advance, empty_pair(src_tiles), slot_ids)
        return result

    def col_sweep(src_pot):
        def advance(totals, slot_index):
            cost_tile = tile_cost[slot_index].astype(jnp.float32)
            src_tile = tile_pairs[slot_index, 0].astype(jnp.int32)
            tgt_tile = tile_pairs[slot_index, 1].astype(jnp.int32)
            row_pot = lax.dynamic_slice_in_dim(src_pot, src_tile * edge, edge)
            scores = (row_pot[:, None] - cost_tile) / entropic
            maxima = jnp.max(scores, axis=0)
            sums = jnp.sum(jnp.exp(scores - maxima[None, :]), axis=0)
            maxima = jnp.where(alive[slot_index], maxima, negative_floor)
            sums = jnp.where(alive[slot_index], sums, 0.0)
            return merge_into(totals, tgt_tile, (maxima, sums)), None
        result, unused = lax.scan(advance, empty_pair(tgt_tiles), slot_ids)
        return result

    def map_sweep(src_pot, tgt_pot):
        def advance(totals, slot_index):
            numer, denom = totals
            cost_tile = tile_cost[slot_index].astype(jnp.float32)
            src_tile = tile_pairs[slot_index, 0].astype(jnp.int32)
            tgt_tile = tile_pairs[slot_index, 1].astype(jnp.int32)
            row_pot = lax.dynamic_slice_in_dim(src_pot, src_tile * edge, edge)
            column_pot = lax.dynamic_slice_in_dim(tgt_pot, tgt_tile * edge, edge)
            weights = jnp.exp((row_pot[:, None] + column_pot[None, :] - cost_tile) / entropic)
            weights = jnp.where(alive[slot_index], weights, 0.0)
            old_mass = lax.dynamic_index_in_dim(denom, src_tile, 0, False)
            denom = lax.dynamic_update_index_in_dim(denom, old_mass + jnp.sum(weights, axis=1), src_tile, 0)
            columns = lax.dynamic_slice_in_dim(targets_t, tgt_tile * edge, edge, 1)
            part = lax.dot_general(columns, weights.astype(jnp.bfloat16), (((1,), (1,)), ((), ())), preferred_element_type=jnp.float32)
            current = lax.dynamic_slice_in_dim(numer, src_tile * edge, edge, 1)
            numer = lax.dynamic_update_slice_in_dim(numer, current + part, src_tile * edge, 1)
            return (numer, denom), None
        start = (jnp.zeros((targets_t.shape[0], src_mass.shape[0]), jnp.float32), jnp.zeros((src_tiles, edge), jnp.float32))
        result, unused = lax.scan(advance, start, slot_ids)
        return result

    tgt_pot = jnp.zeros(tgt_mass.shape, jnp.float32)
    src_pot = jnp.zeros(src_mass.shape, jnp.float32)
    for repeat_index in range(ITERS):
        src_pot = potential(row_sweep(tgt_pot), src_mass)
        tgt_pot = potential(col_sweep(src_pot), tgt_mass)
    numer, denom = map_sweep(src_pot, tgt_pot)
    return numer / denom.reshape(-1)[None, :]
```

```python
import functools

import jax
import jax.numpy as jnp
from jax import lax
from jax.experimental import pallas as pl
from jax.experimental.pallas import tpu as pltpu
from jax.sharding import PartitionSpec as P

MESH = pl.DeviceIdType.MESH
inverse_eps = 50.0
negative_floor = -1e30
ROWS = 64
LANES = 128
PAD = 16


def logsumexp0(parts):
    top = jnp.max(parts, axis=0)
    return top + jnp.log(jnp.sum(jnp.exp(parts - top[None]), axis=0))


def kernel(
    n_src,
    n_tgt,
    pairs_ref,
    count_ref,
    cost_hbm,
    src_mass_ref,
    tgt_mass_ref,
    targets_hbm,
    out_ref,
    cost,
    q,
    tgts,
    prods,
    slot_cols,
    slot_rows,
    pad_rows,
    row_pot,
    col_stab,
    col_sum,
    col_fac,
    tgt_pot,
    row_buf1,
    row_buf2,
    col_buf1,
    col_buf2,
    out_send,
    out_recv,
    cost_sem,
    tgts_sem,
    row_send1,
    row_recv1,
    row_send2,
    row_recv2,
    col_send1,
    col_recv1,
    col_send2,
    col_recv2,
    out_send_sem,
    out_recv_sem,
):
    cap, edge = cost.shape[0], cost.shape[1]
    src_tiles, tgt_tiles = src_mass_ref.shape[0], tgt_mass_ref.shape[0]
    dim = targets_hbm.shape[0]
    my_src, my_tgt = lax.axis_index("src"), lax.axis_index("tgt")
    chunks = edge // ROWS

    for k in range(cap):
        pltpu.make_async_copy(cost_hbm.at[k], cost.at[k], cost_sem.at[k]).start()
    for t in range(tgt_tiles):
        pltpu.make_async_copy(
            targets_hbm.at[:, pl.ds(t * edge, edge)], tgts.at[t, pl.ds(0, dim)], tgts_sem.at[t]
        ).start()

    barrier = pltpu.get_barrier_semaphore()
    for off in range(1, n_tgt):
        pl.semaphore_signal(
            barrier, inc=1, device_id={"tgt": lax.rem(my_tgt + off, n_tgt)}, device_id_type=MESH
        )
    for off in range(1, n_src):
        pl.semaphore_signal(
            barrier, inc=1, device_id={"src": lax.rem(my_src + off, n_src)}, device_id_type=MESH
        )

    pad_rows[...] = jnp.zeros_like(pad_rows)
    slot_cols[...] = jnp.zeros_like(slot_cols)
    tgts[:, dim:, :] = jnp.ones((tgt_tiles, PAD, edge), jnp.bfloat16)

    count = count_ref[0]
    src_of = [lax.rem(pairs_ref[k, 0], src_tiles) for k in range(cap)]
    tgt_of = [lax.rem(pairs_ref[k, 1], tgt_tiles) for k in range(cap)]
    src_id = [jnp.where(k < count, src_of[k], -1) for k in range(cap)]
    tgt_id = [jnp.where(k < count, tgt_of[k], -1) for k in range(cap)]
    src_rows = lax.broadcasted_iota(jnp.int32, (src_tiles, edge), 0)
    tgt_rows = lax.broadcasted_iota(jnp.int32, (tgt_tiles, edge), 0)
    lane = lax.broadcasted_iota(jnp.int32, (ROWS, LANES), 1)

    def wide(block):
        return jnp.concatenate([block] * (edge // LANES), axis=1)

    def put_column(k, c, value):
        rows = slice(c * ROWS, (c + 1) * ROWS)
        slot_cols[rows, :] = jnp.where(lane == k, value, slot_cols[rows, :])

    def slots_as_rows():
        slot_rows[...] = slot_cols[...].T[:PAD]

    def spread_rows(values):
        pad_rows[0:src_tiles, :] = values
        columns = pad_rows[...].T
        for s in range(src_tiles):
            row_pot[s] = jnp.broadcast_to(columns[:, s : s + 1], (edge, LANES))

    def exchange(buf, axis, me, n, send_sem, recv_sem):
        copies = []
        for off in range(1, n):
            copy = pltpu.make_async_remote_copy(
                src_ref=buf.at[0],
                dst_ref=buf.at[off],
                send_sem=send_sem.at[off - 1],
                recv_sem=recv_sem.at[off - 1],
                device_id={axis: lax.rem(me + off, n)},
                device_id_type=MESH,
            )
            copy.start()
            copies.append(copy)
        for copy in copies:
            copy.wait()

    def merge_logs(parts, ids, rows):
        top = jnp.full(rows.shape, negative_floor, jnp.float32)
        for part, tile in zip(parts, ids):
            top = jnp.maximum(top, jnp.where(rows == tile, part, negative_floor))
        total = jnp.zeros(rows.shape, jnp.float32)
        for part, tile in zip(parts, ids):
            total = total + jnp.where(rows == tile, jnp.exp(part - top), 0.0)
        return jnp.where(total > 0.0, top + jnp.log(total), negative_floor)

    def merge_sums(parts, ids, rows):
        total = jnp.zeros(rows.shape, jnp.float32)
        for part, tile in zip(parts, ids):
            total = total + jnp.where(rows == tile, part, 0.0)
        return total

    def row_first(k, carry):
        pltpu.make_async_copy(cost_hbm.at[k], cost.at[k], cost_sem.at[k]).wait()
        for c in range(chunks):
            tile = cost[k, c * ROWS : (c + 1) * ROWS, :].astype(jnp.float32)
            low = jnp.min(tile, axis=1, keepdims=True)
            total = jnp.sum(jnp.exp((low - tile) * inverse_eps), axis=1, keepdims=True)
            put_column(k, c, jnp.log(total) - low * inverse_eps)
        return carry

    lax.fori_loop(0, cap, row_first, 0)
    slots_as_rows()
    row_buf1[0] = merge_logs([slot_rows[k : k + 1, :] for k in range(cap)], src_id, src_rows)
    pl.semaphore_wait(barrier, n_tgt - 1 + n_src - 1)
    exchange(row_buf1, "tgt", my_tgt, n_tgt, row_send1, row_recv1)
    spread_rows(jnp.log(src_mass_ref[...]) - logsumexp0(row_buf1[...]))

    def col_first(k, carry):
        s = lax.rem(pairs_ref[k, 0], src_tiles)
        top = jnp.full((8, edge), negative_floor, jnp.float32)
        for c in range(chunks):
            rows = slice(c * ROWS, (c + 1) * ROWS)
            score = wide(row_pot[s, rows, :]) - cost[k, rows, :].astype(jnp.float32) * inverse_eps
            q[k, rows, :] = score
            top = jnp.maximum(top, jnp.max(score.reshape(ROWS // 8, 8, edge), axis=0))
        top = jnp.broadcast_to(jnp.max(top, axis=0, keepdims=True), (8, edge))
        total = jnp.zeros((8, edge), jnp.float32)
        for c in range(chunks):
            rows = slice(c * ROWS, (c + 1) * ROWS)
            value = jnp.exp(q[k, rows, :].reshape(ROWS // 8, 8, edge) - top[None])
            q[k, rows, :] = value.reshape(ROWS, edge)
            total = total + jnp.sum(value, axis=0)
        col_stab[k] = top
        col_sum[k] = jnp.broadcast_to(jnp.sum(total, axis=0, keepdims=True), (8, edge))
        return carry

    lax.fori_loop(0, cap, col_first, 0)
    col_buf1[0] = merge_logs(
        [col_stab[k, 0:1, :] + jnp.log(col_sum[k, 0:1, :]) for k in range(cap)], tgt_id, tgt_rows
    )
    exchange(col_buf1, "src", my_src, n_src, col_send1, col_recv1)
    potential = jnp.log(tgt_mass_ref[...]) - logsumexp0(col_buf1[...])
    for t in range(tgt_tiles):
        tgt_pot[t] = jnp.broadcast_to(potential[t : t + 1, :], (8, edge))

    def row_second(k, carry):
        t = lax.rem(pairs_ref[k, 1], tgt_tiles)
        alive = jnp.full((8, edge), k, jnp.int32) < count
        factor = jnp.where(alive, jnp.exp(tgt_pot[t] + col_stab[k]), 0.0)
        col_fac[k] = factor
        for c in range(chunks):
            rows = slice(c * ROWS, (c + 1) * ROWS)
            value = q[k, rows, :].reshape(ROWS // 8, 8, edge) * factor[None]
            put_column(k, c, jnp.sum(value.reshape(ROWS, edge), axis=1, keepdims=True))
        return carry

    lax.fori_loop(0, cap, row_second, 0)
    slots_as_rows()
    row_buf2[0] = merge_sums([slot_rows[k : k + 1, :] for k in range(cap)], src_id, src_rows)
    exchange(row_buf2, "tgt", my_tgt, n_tgt, row_send2, row_recv2)
    spread_rows(src_mass_ref[...] / jnp.sum(row_buf2[...], axis=0))

    def col_second(k, carry):
        s = lax.rem(pairs_ref[k, 0], src_tiles)
        total = jnp.zeros((8, edge), jnp.float32)
        for c in range(chunks):
            rows = slice(c * ROWS, (c + 1) * ROWS)
            value = q[k, rows, :] * wide(row_pot[s, rows, :])
            total = total + jnp.sum(value.reshape(ROWS // 8, 8, edge), axis=0)
        col_sum[k] = jnp.broadcast_to(jnp.sum(total, axis=0, keepdims=True), (8, edge)) * col_fac[k]
        return carry

    lax.fori_loop(0, cap, col_second, 0)
    col_buf2[0] = merge_sums([col_sum[k, 0:1, :] for k in range(cap)], tgt_id, tgt_rows)
    exchange(col_buf2, "src", my_src, n_src, col_send2, col_recv2)
    potential = tgt_mass_ref[...] / jnp.sum(col_buf2[...], axis=0)
    for t in range(tgt_tiles):
        tgt_pot[t] = jnp.broadcast_to(potential[t : t + 1, :], (8, edge))

    for t in range(tgt_tiles):
        pltpu.make_async_copy(
            targets_hbm.at[:, pl.ds(t * edge, edge)], tgts.at[t, pl.ds(0, dim)], tgts_sem.at[t]
        ).wait()

    def map_slot(k, carry):
        s = lax.rem(pairs_ref[k, 0], src_tiles)
        t = lax.rem(pairs_ref[k, 1], tgt_tiles)
        factor = tgt_pot[t] * col_fac[k]
        left = tgts[t]
        for h in range(edge // 256):
            parts = []
            for c in range(256 // ROWS):
                rows = slice(h * 256 + c * ROWS, h * 256 + (c + 1) * ROWS)
                value = (q[k, rows, :] * wide(row_pot[s, rows, :])).reshape(ROWS // 8, 8, edge)
                parts.append((value * factor[None]).reshape(ROWS, edge).astype(jnp.bfloat16))
            prods[k, :, h * 256 : (h + 1) * 256] = lax.dot_general(
                left,
                jnp.concatenate(parts, axis=0),
                (((1,), (1,)), ((), ())),
                preferred_element_type=jnp.float32,
            )
        return carry

    lax.fori_loop(0, cap, map_slot, 0)

    share = out_ref.shape[1]
    tall = dim + PAD
    low_half = lax.broadcasted_iota(jnp.int32, (tall, LANES), 0) >= dim + PAD // 2
    for s in range(src_tiles):
        picks = [jnp.where(src_id[k] == s, 1.0, 0.0) for k in range(cap)]
        for c in range(edge // LANES):
            total = jnp.zeros((tall, LANES), jnp.float32)
            for k in range(cap):
                total = total + prods[k, :, c * LANES : (c + 1) * LANES] * picks[k]
            rest = total - total.astype(jnp.bfloat16).astype(jnp.float32)
            total = jnp.where(low_half, rest, total)
            place = s * edge + c * LANES
            start = place % share
            out_send[place // share, :, start : start + LANES] = total.astype(jnp.bfloat16)

    copies = []
    for off in range(1, n_tgt):
        peer = lax.rem(my_tgt + off, n_tgt)
        copy = pltpu.make_async_remote_copy(
            src_ref=out_send.at[peer],
            dst_ref=out_recv.at[off - 1],
            send_sem=out_send_sem.at[off - 1],
            recv_sem=out_recv_sem.at[off - 1],
            device_id={"tgt": peer},
            device_id_type=MESH,
        )
        copy.start()
        copies.append(copy)
    total = out_send[my_tgt].astype(jnp.float32)
    for off, copy in enumerate(copies):
        copy.wait()
        total = total + out_recv[off].astype(jnp.float32)
    mass = total[dim : dim + 1] + total[dim + PAD // 2 : dim + PAD // 2 + 1]
    out_ref[...] = total[:dim] / mass


def local(n_src, n_tgt, tile_cost, tile_pairs, tile_counts, src_mass, tgt_mass, targets_t):
    cap, edge = tile_cost.shape[0], tile_cost.shape[1]
    src_tiles, tgt_tiles = src_mass.shape[0] // edge, tgt_mass.shape[0] // edge
    dim = targets_t.shape[0]
    share = src_mass.shape[0] // n_tgt
    tall = dim + PAD
    f32, bf16 = jnp.float32, jnp.bfloat16
    dma = pltpu.SemaphoreType.DMA
    smem = pl.BlockSpec(memory_space=pltpu.SMEM)
    vmem = pl.BlockSpec(memory_space=pltpu.VMEM)
    hbm = pl.BlockSpec(memory_space=pl.ANY)
    return pl.pallas_call(
        functools.partial(kernel, n_src, n_tgt),
        out_shape=jax.ShapeDtypeStruct((dim, share), f32),
        in_specs=[smem, smem, hbm, vmem, vmem, hbm],
        out_specs=vmem,
        scratch_shapes=[
            pltpu.VMEM((cap, edge, edge), bf16),
            pltpu.VMEM((cap, edge, edge), f32),
            pltpu.VMEM((tgt_tiles, tall, edge), bf16),
            pltpu.VMEM((cap, tall, edge), f32),
            pltpu.VMEM((edge, LANES), f32),
            pltpu.VMEM((PAD, edge), f32),
            pltpu.VMEM((LANES, edge), f32),
            pltpu.VMEM((src_tiles, edge, LANES), f32),
            pltpu.VMEM((cap, 8, edge), f32),
            pltpu.VMEM((cap, 8, edge), f32),
            pltpu.VMEM((cap, 8, edge), f32),
            pltpu.VMEM((tgt_tiles, 8, edge), f32),
            pltpu.VMEM((n_tgt, src_tiles, edge), f32),
            pltpu.VMEM((n_tgt, src_tiles, edge), f32),
            pltpu.VMEM((n_src, tgt_tiles, edge), f32),
            pltpu.VMEM((n_src, tgt_tiles, edge), f32),
            pltpu.VMEM((n_tgt, tall, share), bf16),
            pltpu.VMEM((n_tgt - 1, tall, share), bf16),
            dma((cap,)),
            dma((tgt_tiles,)),
            dma((n_tgt - 1,)),
            dma((n_tgt - 1,)),
            dma((n_tgt - 1,)),
            dma((n_tgt - 1,)),
            dma((n_src - 1,)),
            dma((n_src - 1,)),
            dma((n_src - 1,)),
            dma((n_src - 1,)),
            dma((n_tgt - 1,)),
            dma((n_tgt - 1,)),
        ],
        compiler_params=pltpu.CompilerParams(
            collective_id=0, has_side_effects=True, vmem_limit_bytes=56 * 1024 * 1024
        ),
    )(
        tile_pairs,
        tile_counts,
        tile_cost,
        src_mass.reshape(src_tiles, edge),
        tgt_mass.reshape(tgt_tiles, edge),
        targets_t,
    )


def solution(mesh):
    return jax.shard_map(
        functools.partial(local, mesh.shape["src"], mesh.shape["tgt"]),
        mesh=mesh,
        in_specs=(
            P(("src", "tgt"), None, None),
            P(("src", "tgt"), None),
            P(("src", "tgt")),
            P("src"),
            P("tgt"),
            P(None, "tgt"),
        ),
        out_specs=P(None, ("src", "tgt")),
        check_vma=False,
    )
```

```python
import functools

import jax
import jax.numpy as jnp
from jax import lax
from jax.experimental import pallas as pl
from jax.experimental.pallas import tpu as pltpu
from jax.sharding import PartitionSpec as P

MESH = pl.DeviceIdType.MESH
inverse_eps = 50.0 * 1.4426950408889634
negative_floor = -1e30
ROWS = 64
LANES = 128
PAD = 16


def logsumexp0(parts):
    top = jnp.max(parts, axis=0)
    return top + jnp.log2(jnp.sum(jnp.exp2(parts - top[None]), axis=0))


def kernel(
    n_src,
    n_tgt,
    pairs_ref,
    count_ref,
    cost_hbm,
    src_mass_flat,
    tgt_mass_flat,
    targets_hbm,
    out_ref,
    cost,
    q,
    tgts,
    prods,
    slot_cols,
    slot_rows,
    pad_rows,
    row_pot,
    col_stab,
    col_sum,
    col_fac,
    tgt_pot,
    src_mass_ref,
    tgt_mass_ref,
    row_buf1,
    row_buf2,
    col_buf1,
    col_buf2,
    out_part,
    pair_recv,
    out_send,
    out_recv,
    cost_sem,
    tgts_sem,
    row_send1,
    row_recv1,
    row_send2,
    row_recv2,
    col_send1,
    col_recv1,
    col_send2,
    col_recv2,
    pair_send_sem,
    pair_recv_sem,
    out_send_sem,
    out_recv_sem,
):
    cap, edge = cost.shape[0], cost.shape[1]
    src_tiles, tgt_tiles = src_mass_ref.shape[0], tgt_mass_ref.shape[0]
    dim = targets_hbm.shape[0]
    my_src, my_tgt = lax.axis_index("src"), lax.axis_index("tgt")
    chunks = edge // ROWS

    for k in range(cap):
        pltpu.make_async_copy(cost_hbm.at[k], cost.at[k], cost_sem.at[k]).start()
    for t in range(tgt_tiles):
        pltpu.make_async_copy(
            targets_hbm.at[:, pl.ds(t * edge, edge)], tgts.at[t, pl.ds(0, dim)], tgts_sem.at[t]
        ).start()

    barrier = pltpu.get_barrier_semaphore()
    for off in range(1, n_tgt):
        pl.semaphore_signal(
            barrier, inc=1, device_id={"tgt": lax.rem(my_tgt + off, n_tgt)}, device_id_type=MESH
        )
    for off in range(1, n_src):
        pl.semaphore_signal(
            barrier, inc=1, device_id={"src": lax.rem(my_src + off, n_src)}, device_id_type=MESH
        )

    pad_rows[...] = jnp.zeros_like(pad_rows)
    slot_cols[...] = jnp.zeros_like(slot_cols)
    tgts[:, dim:, :] = jnp.ones((tgt_tiles, PAD, edge), jnp.bfloat16)

    for s in range(src_tiles):
        src_mass_ref[s : s + 1, :] = src_mass_flat[s * edge : (s + 1) * edge].reshape(1, edge)
    for t in range(tgt_tiles):
        tgt_mass_ref[t : t + 1, :] = tgt_mass_flat[t * edge : (t + 1) * edge].reshape(1, edge)

    count = count_ref[0]
    src_of = [lax.rem(pairs_ref[0, k], src_tiles) for k in range(cap)]
    tgt_of = [lax.rem(pairs_ref[1, k], tgt_tiles) for k in range(cap)]
    src_id = [jnp.where(k < count, src_of[k], -1) for k in range(cap)]
    tgt_id = [jnp.where(k < count, tgt_of[k], -1) for k in range(cap)]
    src_rows = lax.broadcasted_iota(jnp.int32, (src_tiles, edge), 0)
    tgt_rows = lax.broadcasted_iota(jnp.int32, (tgt_tiles, edge), 0)
    lane = lax.broadcasted_iota(jnp.int32, (ROWS, LANES), 1)

    def wide(block):
        return jnp.concatenate([block] * (edge // LANES), axis=1)

    def put_column(k, c, value):
        rows = slice(c * ROWS, (c + 1) * ROWS)
        slot_cols[rows, :] = jnp.where(lane == k, value, slot_cols[rows, :])

    def slots_as_rows():
        slot_rows[...] = slot_cols[...].T[:PAD]

    def spread_rows(values):
        pad_rows[0:src_tiles, :] = values
        columns = pad_rows[...].T
        for s in range(src_tiles):
            row_pot[s] = jnp.broadcast_to(columns[:, s : s + 1], (edge, LANES))

    def exchange(buf, axis, me, n, send_sem, recv_sem):
        copies = []
        for off in range(1, n):
            copy = pltpu.make_async_remote_copy(
                src_ref=buf.at[0],
                dst_ref=buf.at[off],
                send_sem=send_sem.at[off - 1],
                recv_sem=recv_sem.at[off - 1],
                device_id={axis: lax.rem(me + off, n)},
                device_id_type=MESH,
            )
            copy.start()
            copies.append(copy)
        for copy in copies:
            copy.wait()

    def merge_logs(parts, ids, rows):
        top = jnp.full(rows.shape, negative_floor, jnp.float32)
        for part, tile in zip(parts, ids):
            top = jnp.maximum(top, jnp.where(rows == tile, part, negative_floor))
        total = jnp.zeros(rows.shape, jnp.float32)
        for part, tile in zip(parts, ids):
            total = total + jnp.where(rows == tile, jnp.exp2(part - top), 0.0)
        return jnp.where(total > 0.0, top + jnp.log2(total), negative_floor)

    def merge_sums(parts, ids, rows):
        total = jnp.zeros(rows.shape, jnp.float32)
        for part, tile in zip(parts, ids):
            total = total + jnp.where(rows == tile, part, 0.0)
        return total

    def row_first(k, carry):
        pltpu.make_async_copy(cost_hbm.at[k], cost.at[k], cost_sem.at[k]).wait()
        for c in range(chunks):
            rows = slice(c * ROWS, (c + 1) * ROWS)
            tile = cost[k, rows, :].astype(jnp.float32) * inverse_eps
            q[k, rows, :] = tile
            low = jnp.min(tile, axis=1, keepdims=True)
            total = jnp.sum(jnp.exp2(low - tile), axis=1, keepdims=True)
            put_column(k, c, jnp.log2(total) - low)
        return carry

    lax.fori_loop(0, cap, row_first, 0)
    slots_as_rows()
    row_buf1[0] = merge_logs([slot_rows[k : k + 1, :] for k in range(cap)], src_id, src_rows)
    pl.semaphore_wait(barrier, n_tgt - 1 + n_src - 1)
    exchange(row_buf1, "tgt", my_tgt, n_tgt, row_send1, row_recv1)
    spread_rows(jnp.log2(src_mass_ref[...]) - logsumexp0(row_buf1[...]))

    def col_first(k, carry):
        s = lax.rem(pairs_ref[0, k], src_tiles)
        top = jnp.full((8, edge), negative_floor, jnp.float32)
        for c in range(chunks):
            rows = slice(c * ROWS, (c + 1) * ROWS)
            score = wide(row_pot[s, rows, :]) - q[k, rows, :]
            q[k, rows, :] = score
            top = jnp.maximum(top, jnp.max(score.reshape(ROWS // 8, 8, edge), axis=0))
        top = jnp.broadcast_to(jnp.max(top, axis=0, keepdims=True), (8, edge))
        total = jnp.zeros((8, edge), jnp.float32)
        for c in range(chunks):
            rows = slice(c * ROWS, (c + 1) * ROWS)
            value = jnp.exp2(q[k, rows, :].reshape(ROWS // 8, 8, edge) - top[None])
            q[k, rows, :] = value.reshape(ROWS, edge)
            total = total + jnp.sum(value, axis=0)
        col_stab[k] = top
        col_sum[k] = jnp.broadcast_to(jnp.sum(total, axis=0, keepdims=True), (8, edge))
        return carry

    lax.fori_loop(0, cap, col_first, 0)
    col_buf1[0] = merge_logs(
        [col_stab[k, 0:1, :] + jnp.log2(col_sum[k, 0:1, :]) for k in range(cap)], tgt_id, tgt_rows
    )
    exchange(col_buf1, "src", my_src, n_src, col_send1, col_recv1)
    potential = jnp.log2(tgt_mass_ref[...]) - logsumexp0(col_buf1[...])
    for t in range(tgt_tiles):
        tgt_pot[t] = jnp.broadcast_to(potential[t : t + 1, :], (8, edge))

    def row_second(k, carry):
        t = lax.rem(pairs_ref[1, k], tgt_tiles)
        alive = jnp.full((8, edge), k, jnp.int32) < count
        factor = jnp.where(alive, jnp.exp2(tgt_pot[t] + col_stab[k]), 0.0)
        col_fac[k] = factor
        for c in range(chunks):
            rows = slice(c * ROWS, (c + 1) * ROWS)
            value = q[k, rows, :].reshape(ROWS // 8, 8, edge) * factor[None]
            put_column(k, c, jnp.sum(value.reshape(ROWS, edge), axis=1, keepdims=True))
        return carry

    lax.fori_loop(0, cap, row_second, 0)
    slots_as_rows()
    row_buf2[0] = merge_sums([slot_rows[k : k + 1, :] for k in range(cap)], src_id, src_rows)
    exchange(row_buf2, "tgt", my_tgt, n_tgt, row_send2, row_recv2)
    spread_rows(src_mass_ref[...] / jnp.sum(row_buf2[...], axis=0))

    def col_second(k, carry):
        s = lax.rem(pairs_ref[0, k], src_tiles)
        total = jnp.zeros((8, edge), jnp.float32)
        for c in range(chunks):
            rows = slice(c * ROWS, (c + 1) * ROWS)
            value = q[k, rows, :] * wide(row_pot[s, rows, :])
            total = total + jnp.sum(value.reshape(ROWS // 8, 8, edge), axis=0)
        col_sum[k] = jnp.broadcast_to(jnp.sum(total, axis=0, keepdims=True), (8, edge)) * col_fac[k]
        return carry

    lax.fori_loop(0, cap, col_second, 0)
    col_buf2[0] = merge_sums([col_sum[k, 0:1, :] for k in range(cap)], tgt_id, tgt_rows)
    exchange(col_buf2, "src", my_src, n_src, col_send2, col_recv2)
    potential = tgt_mass_ref[...] / jnp.sum(col_buf2[...], axis=0)
    for t in range(tgt_tiles):
        tgt_pot[t] = jnp.broadcast_to(potential[t : t + 1, :], (8, edge))

    for t in range(tgt_tiles):
        pltpu.make_async_copy(
            targets_hbm.at[:, pl.ds(t * edge, edge)], tgts.at[t, pl.ds(0, dim)], tgts_sem.at[t]
        ).wait()

    def map_slot(k, carry):
        s = lax.rem(pairs_ref[0, k], src_tiles)
        t = lax.rem(pairs_ref[1, k], tgt_tiles)
        factor = tgt_pot[t] * col_fac[k]
        left = tgts[t]
        for h in range(edge // 256):
            parts = []
            for c in range(256 // ROWS):
                rows = slice(h * 256 + c * ROWS, h * 256 + (c + 1) * ROWS)
                value = (q[k, rows, :] * wide(row_pot[s, rows, :])).reshape(ROWS // 8, 8, edge)
                parts.append((value * factor[None]).reshape(ROWS, edge).astype(jnp.bfloat16))
            prods[k, :, h * 256 : (h + 1) * 256] = lax.dot_general(
                left,
                jnp.concatenate(parts, axis=0),
                (((1,), (1,)), ((), ())),
                preferred_element_type=jnp.float32,
            )
        return carry

    lax.fori_loop(0, cap, map_slot, 0)

    share = out_ref.shape[1]
    tall = dim + PAD
    core, layer, layers = lax.rem(my_tgt, 2), my_tgt // 2, n_tgt // 2

    def pair_copy(j):
        return pltpu.make_async_remote_copy(
            src_ref=out_part.at[2 * j + 1 - core],
            dst_ref=pair_recv.at[j],
            send_sem=pair_send_sem.at[j],
            recv_sem=pair_recv_sem.at[j],
            device_id={"tgt": my_tgt + 1 - 2 * core},
            device_id_type=MESH,
        )

    picks = [
        [jnp.where(src_id[k] == s, 1.0, 0.0) for k in range(cap)] for s in range(src_tiles)
    ]
    for place in range(0, src_tiles * edge, LANES):
        s, start = place // edge, place % edge
        total = jnp.zeros((tall, LANES), jnp.float32)
        for k in range(cap):
            total = total + prods[k, :, start : start + LANES] * picks[s][k]
        block, start = place // share, place % share
        out_part[block, :, start : start + LANES] = total
        if (place + LANES) % (2 * share) == 0:
            pair_copy(block // 2).start()

    low_half = lax.broadcasted_iota(jnp.int32, (tall, share), 0) >= dim + PAD // 2
    copies = []
    for off in range(1, layers):
        other = lax.rem(layer + off, layers)
        pair_copy(other).wait()
        total = out_part[2 * other + core] + pair_recv[other]
        rest = total - total.astype(jnp.bfloat16).astype(jnp.float32)
        out_send[off - 1] = jnp.where(low_half, rest, total).astype(jnp.bfloat16)
        copy = pltpu.make_async_remote_copy(
            src_ref=out_send.at[off - 1],
            dst_ref=out_recv.at[off - 1],
            send_sem=out_send_sem.at[off - 1],
            recv_sem=out_recv_sem.at[off - 1],
            device_id={"tgt": 2 * other + core},
            device_id_type=MESH,
        )
        copy.start()
        copies.append(copy)
    pair_copy(layer).wait()
    total = out_part[2 * layer + core] + pair_recv[layer]
    total = jnp.where(low_half, 0.0, total)
    for off, copy in enumerate(copies):
        copy.wait()
        total = total + out_recv[off].astype(jnp.float32)
    mass = total[dim : dim + 1] + total[dim + PAD // 2 : dim + PAD // 2 + 1]
    out_ref[...] = total[:dim] / mass


def local(n_src, n_tgt, tile_cost, tile_pairs, tile_counts, src_mass, tgt_mass, targets_t):
    cap, edge = tile_cost.shape[0], tile_cost.shape[1]
    src_tiles, tgt_tiles = src_mass.shape[0] // edge, tgt_mass.shape[0] // edge
    dim = targets_t.shape[0]
    share = src_mass.shape[0] // n_tgt
    tall = dim + PAD
    f32, bf16 = jnp.float32, jnp.bfloat16
    dma = pltpu.SemaphoreType.DMA
    smem = pl.BlockSpec(memory_space=pltpu.SMEM)
    vmem = pl.BlockSpec(memory_space=pltpu.VMEM)
    hbm = pl.BlockSpec(memory_space=pl.ANY)
    return pl.pallas_call(
        functools.partial(kernel, n_src, n_tgt),
        out_shape=jax.ShapeDtypeStruct((dim, share), f32),
        in_specs=[smem, smem, hbm, vmem, vmem, hbm],
        out_specs=vmem,
        scratch_shapes=[
            pltpu.VMEM((cap, edge, edge), bf16),
            pltpu.VMEM((cap, edge, edge), f32),
            pltpu.VMEM((tgt_tiles, tall, edge), bf16),
            pltpu.VMEM((cap, tall, edge), f32),
            pltpu.VMEM((edge, LANES), f32),
            pltpu.VMEM((PAD, edge), f32),
            pltpu.VMEM((LANES, edge), f32),
            pltpu.VMEM((src_tiles, edge, LANES), f32),
            pltpu.VMEM((cap, 8, edge), f32),
            pltpu.VMEM((cap, 8, edge), f32),
            pltpu.VMEM((cap, 8, edge), f32),
            pltpu.VMEM((tgt_tiles, 8, edge), f32),
            pltpu.VMEM((src_tiles, edge), f32),
            pltpu.VMEM((tgt_tiles, edge), f32),
            pltpu.VMEM((n_tgt, src_tiles, edge), f32),
            pltpu.VMEM((n_tgt, src_tiles, edge), f32),
            pltpu.VMEM((n_src, tgt_tiles, edge), f32),
            pltpu.VMEM((n_src, tgt_tiles, edge), f32),
            pltpu.VMEM((n_tgt, tall, share), f32),
            pltpu.VMEM((n_tgt // 2, tall, share), f32),
            pltpu.VMEM((n_tgt // 2 - 1, tall, share), bf16),
            pltpu.VMEM((n_tgt // 2 - 1, tall, share), bf16),
            dma((cap,)),
            dma((tgt_tiles,)),
            dma((n_tgt - 1,)),
            dma((n_tgt - 1,)),
            dma((n_tgt - 1,)),
            dma((n_tgt - 1,)),
            dma((n_src - 1,)),
            dma((n_src - 1,)),
            dma((n_src - 1,)),
            dma((n_src - 1,)),
            dma((n_tgt // 2,)),
            dma((n_tgt // 2,)),
            dma((n_tgt // 2 - 1,)),
            dma((n_tgt // 2 - 1,)),
        ],
        compiler_params=pltpu.CompilerParams(
            collective_id=0, has_side_effects=True, vmem_limit_bytes=56 * 1024 * 1024
        ),
    )(
        tile_pairs.T,
        tile_counts,
        tile_cost,
        src_mass,
        tgt_mass,
        targets_t,
    )


def solution(mesh):
    return jax.shard_map(
        functools.partial(local, mesh.shape["src"], mesh.shape["tgt"]),
        mesh=mesh,
        in_specs=(
            P(("src", "tgt"), None, None),
            P(("src", "tgt"), None),
            P(("src", "tgt")),
            P("src"),
            P("tgt"),
            P(None, "tgt"),
        ),
        out_specs=P(None, ("src", "tgt")),
        check_vma=False,
    )
```

```python
import functools

import jax
import jax.numpy as jnp
from jax import lax
from jax.experimental import pallas as pl
from jax.experimental.pallas import tpu as pltpu
from jax.sharding import PartitionSpec as P

MESH = pl.DeviceIdType.MESH
inverse_eps = 50.0 * 1.4426950408889634
negative_floor = -1e30
ROWS = 64
LANES = 128
PAD = 16


def logsumexp0(parts):
    top = jnp.max(parts, axis=0)
    return top + jnp.log2(jnp.sum(jnp.exp2(parts - top[None]), axis=0))


def kernel(
    n_src,
    n_tgt,
    pairs_ref,
    count_ref,
    cost_hbm,
    src_mass_flat,
    tgt_mass_flat,
    targets_hbm,
    out_ref,
    cost,
    q,
    low,
    tgts,
    prods,
    slot_cols,
    slot_rows,
    pad_rows,
    row_pot,
    col_stab,
    col_sum,
    col_fac,
    tgt_pot,
    src_mass_ref,
    tgt_mass_ref,
    row_buf1,
    row_buf2,
    col_buf1,
    col_buf2,
    out_part,
    pair_recv,
    out_send,
    out_recv,
    cost_sem,
    tgts_sem,
    row_send1,
    row_recv1,
    row_send2,
    row_recv2,
    col_send1,
    col_recv1,
    col_send2,
    col_recv2,
    pair_send_sem,
    pair_recv_sem,
    out_send_sem,
    out_recv_sem,
):
    cap, edge = cost.shape[0], cost.shape[1]
    src_tiles, tgt_tiles = src_mass_ref.shape[0], tgt_mass_ref.shape[0]
    dim = targets_hbm.shape[0]
    my_src, my_tgt = lax.axis_index("src"), lax.axis_index("tgt")
    chunks = edge // ROWS

    for k in range(cap):
        pltpu.make_async_copy(cost_hbm.at[k], cost.at[k], cost_sem.at[k]).start()
    for t in range(tgt_tiles):
        pltpu.make_async_copy(
            targets_hbm.at[:, pl.ds(t * edge, edge)], tgts.at[t, pl.ds(0, dim)], tgts_sem.at[t]
        ).start()

    barrier = pltpu.get_barrier_semaphore()
    for off in range(1, n_tgt):
        pl.semaphore_signal(
            barrier, inc=1, device_id={"tgt": lax.rem(my_tgt + off, n_tgt)}, device_id_type=MESH
        )
    for off in range(1, n_src):
        pl.semaphore_signal(
            barrier, inc=1, device_id={"src": lax.rem(my_src + off, n_src)}, device_id_type=MESH
        )

    pad_rows[...] = jnp.zeros_like(pad_rows)
    slot_cols[...] = jnp.zeros_like(slot_cols)
    tgts[:, dim:, :] = jnp.ones((tgt_tiles, PAD, edge), jnp.bfloat16)

    for s in range(src_tiles):
        src_mass_ref[s : s + 1, :] = src_mass_flat[s * edge : (s + 1) * edge].reshape(1, edge)
    for t in range(tgt_tiles):
        tgt_mass_ref[t : t + 1, :] = tgt_mass_flat[t * edge : (t + 1) * edge].reshape(1, edge)

    count = count_ref[0]
    src_of = [lax.rem(pairs_ref[0, k], src_tiles) for k in range(cap)]
    tgt_of = [lax.rem(pairs_ref[1, k], tgt_tiles) for k in range(cap)]
    src_id = [jnp.where(k < count, src_of[k], -1) for k in range(cap)]
    tgt_id = [jnp.where(k < count, tgt_of[k], -1) for k in range(cap)]
    src_rows = lax.broadcasted_iota(jnp.int32, (src_tiles, edge), 0)
    tgt_rows = lax.broadcasted_iota(jnp.int32, (tgt_tiles, edge), 0)
    lane = lax.broadcasted_iota(jnp.int32, (ROWS, LANES), 1)

    def wide(block):
        return jnp.concatenate([block] * (edge // LANES), axis=1)

    def put_column(k, c, value):
        rows = slice(c * ROWS, (c + 1) * ROWS)
        slot_cols[rows, :] = jnp.where(lane == k, value, slot_cols[rows, :])

    def slots_as_rows():
        slot_rows[...] = slot_cols[...].T[:PAD]

    def spread_rows(values):
        pad_rows[0:src_tiles, :] = values
        columns = pad_rows[...].T
        for s in range(src_tiles):
            row_pot[s] = jnp.broadcast_to(columns[:, s : s + 1], (edge, LANES))

    def exchange(buf, axis, me, n, send_sem, recv_sem):
        copies = []
        for off in range(1, n):
            copy = pltpu.make_async_remote_copy(
                src_ref=buf.at[0],
                dst_ref=buf.at[off],
                send_sem=send_sem.at[off - 1],
                recv_sem=recv_sem.at[off - 1],
                device_id={axis: lax.rem(me + off, n)},
                device_id_type=MESH,
            )
            copy.start()
            copies.append(copy)
        for copy in copies:
            copy.wait()

    def merge_logs(parts, ids, rows):
        top = jnp.full(rows.shape, negative_floor, jnp.float32)
        for part, tile in zip(parts, ids):
            top = jnp.maximum(top, jnp.where(rows == tile, part, negative_floor))
        total = jnp.zeros(rows.shape, jnp.float32)
        for part, tile in zip(parts, ids):
            total = total + jnp.where(rows == tile, jnp.exp2(part - top), 0.0)
        return jnp.where(total > 0.0, top + jnp.log2(total), negative_floor)

    def merge_sums(parts, ids, rows):
        total = jnp.zeros(rows.shape, jnp.float32)
        for part, tile in zip(parts, ids):
            total = total + jnp.where(rows == tile, part, 0.0)
        return total

    def halves(combine, block):
        parts = [block[:, at : at + LANES] for at in range(0, edge, LANES)]
        return functools.reduce(combine, parts)

    def in_pairs(step):
        def both(i, carry):
            step(2 * i)
            step(2 * i + 1)
            return carry

        lax.fori_loop(0, cap // 2, both, 0)

    def row_first(i, carry):
        for u in range(2):
            k = 2 * i + u
            pltpu.make_async_copy(cost_hbm.at[k], cost.at[k], cost_sem.at[k]).wait()
            for c in range(chunks):
                rows = slice(c * ROWS, (c + 1) * ROWS)
                tile = cost[k, rows, :].astype(jnp.float32) * inverse_eps
                q[k, rows, :] = tile
                least = jnp.min(halves(jnp.minimum, tile), axis=1, keepdims=True)
                low[u, rows, :] = jnp.broadcast_to(least, (ROWS, LANES))
        for u in range(2):
            k = 2 * i + u
            for c in range(chunks):
                rows = slice(c * ROWS, (c + 1) * ROWS)
                value = jnp.exp2(wide(low[u, rows, :]) - q[k, rows, :])
                total = jnp.sum(halves(jnp.add, value), axis=1, keepdims=True)
                put_column(k, c, jnp.log2(total) - low[u, rows, :])
        return carry

    lax.fori_loop(0, cap // 2, row_first, 0)
    slots_as_rows()
    row_buf1[0] = merge_logs([slot_rows[k : k + 1, :] for k in range(cap)], src_id, src_rows)
    pl.semaphore_wait(barrier, n_tgt - 1 + n_src - 1)
    exchange(row_buf1, "tgt", my_tgt, n_tgt, row_send1, row_recv1)
    spread_rows(jnp.log2(src_mass_ref[...]) - logsumexp0(row_buf1[...]))

    def col_first(i, carry):
        tops = []
        for u in range(2):
            k = 2 * i + u
            s = lax.rem(pairs_ref[0, k], src_tiles)
            top = jnp.full((8, edge), negative_floor, jnp.float32)
            for c in range(chunks):
                rows = slice(c * ROWS, (c + 1) * ROWS)
                score = wide(row_pot[s, rows, :]) - q[k, rows, :]
                top = jnp.maximum(top, jnp.max(score.reshape(ROWS // 8, 8, edge), axis=0))
            tops.append(jnp.broadcast_to(jnp.max(top, axis=0, keepdims=True), (8, edge)))
        for u in range(2):
            k = 2 * i + u
            s = lax.rem(pairs_ref[0, k], src_tiles)
            total = jnp.zeros((8, edge), jnp.float32)
            for c in range(chunks):
                rows = slice(c * ROWS, (c + 1) * ROWS)
                score = (wide(row_pot[s, rows, :]) - q[k, rows, :]).reshape(ROWS // 8, 8, edge)
                value = jnp.exp2(score - tops[u][None])
                q[k, rows, :] = value.reshape(ROWS, edge)
                total = total + jnp.sum(value, axis=0)
            col_stab[k] = tops[u]
            col_sum[k] = jnp.broadcast_to(jnp.sum(total, axis=0, keepdims=True), (8, edge))
        return carry

    lax.fori_loop(0, cap // 2, col_first, 0)
    col_buf1[0] = merge_logs(
        [col_stab[k, 0:1, :] + jnp.log2(col_sum[k, 0:1, :]) for k in range(cap)], tgt_id, tgt_rows
    )
    exchange(col_buf1, "src", my_src, n_src, col_send1, col_recv1)
    potential = jnp.log2(tgt_mass_ref[...]) - logsumexp0(col_buf1[...])
    for t in range(tgt_tiles):
        tgt_pot[t] = jnp.broadcast_to(potential[t : t + 1, :], (8, edge))

    def row_second(k):
        t = lax.rem(pairs_ref[1, k], tgt_tiles)
        alive = jnp.full((8, edge), k, jnp.int32) < count
        factor = jnp.where(alive, jnp.exp2(tgt_pot[t] + col_stab[k]), 0.0)
        col_fac[k] = factor
        for c in range(chunks):
            rows = slice(c * ROWS, (c + 1) * ROWS)
            value = q[k, rows, :].reshape(ROWS // 8, 8, edge) * factor[None]
            total = halves(jnp.add, value.reshape(ROWS, edge))
            put_column(k, c, jnp.sum(total, axis=1, keepdims=True))

    in_pairs(row_second)
    slots_as_rows()
    row_buf2[0] = merge_sums([slot_rows[k : k + 1, :] for k in range(cap)], src_id, src_rows)
    exchange(row_buf2, "tgt", my_tgt, n_tgt, row_send2, row_recv2)
    spread_rows(src_mass_ref[...] / jnp.sum(row_buf2[...], axis=0))

    def col_second(k):
        s = lax.rem(pairs_ref[0, k], src_tiles)
        total = jnp.zeros((8, edge), jnp.float32)
        for c in range(chunks):
            rows = slice(c * ROWS, (c + 1) * ROWS)
            value = q[k, rows, :] * wide(row_pot[s, rows, :])
            total = total + jnp.sum(value.reshape(ROWS // 8, 8, edge), axis=0)
        col_sum[k] = jnp.broadcast_to(jnp.sum(total, axis=0, keepdims=True), (8, edge)) * col_fac[k]

    in_pairs(col_second)
    col_buf2[0] = merge_sums([col_sum[k, 0:1, :] for k in range(cap)], tgt_id, tgt_rows)
    exchange(col_buf2, "src", my_src, n_src, col_send2, col_recv2)
    potential = tgt_mass_ref[...] / jnp.sum(col_buf2[...], axis=0)
    for t in range(tgt_tiles):
        tgt_pot[t] = jnp.broadcast_to(potential[t : t + 1, :], (8, edge))

    for t in range(tgt_tiles):
        pltpu.make_async_copy(
            targets_hbm.at[:, pl.ds(t * edge, edge)], tgts.at[t, pl.ds(0, dim)], tgts_sem.at[t]
        ).wait()

    def map_slot(k):
        s = lax.rem(pairs_ref[0, k], src_tiles)
        t = lax.rem(pairs_ref[1, k], tgt_tiles)
        factor = tgt_pot[t] * col_fac[k]
        left = tgts[t]
        for h in range(edge // 256):
            parts = []
            for c in range(256 // ROWS):
                rows = slice(h * 256 + c * ROWS, h * 256 + (c + 1) * ROWS)
                value = (q[k, rows, :] * wide(row_pot[s, rows, :])).reshape(ROWS // 8, 8, edge)
                parts.append((value * factor[None]).reshape(ROWS, edge).astype(jnp.bfloat16))
            prods[k, :, h * 256 : (h + 1) * 256] = lax.dot_general(
                left,
                jnp.concatenate(parts, axis=0),
                (((1,), (1,)), ((), ())),
                preferred_element_type=jnp.float32,
            )

    in_pairs(map_slot)

    share = out_ref.shape[1]
    tall = dim + PAD
    core, layer, layers = lax.rem(my_tgt, 2), my_tgt // 2, n_tgt // 2

    def pair_copy(j):
        return pltpu.make_async_remote_copy(
            src_ref=out_part.at[2 * j + 1 - core],
            dst_ref=pair_recv.at[j],
            send_sem=pair_send_sem.at[j],
            recv_sem=pair_recv_sem.at[j],
            device_id={"tgt": my_tgt + 1 - 2 * core},
            device_id_type=MESH,
        )

    picks = [
        [jnp.where(src_id[k] == s, 1.0, 0.0) for k in range(cap)] for s in range(src_tiles)
    ]
    for place in range(0, src_tiles * edge, LANES):
        s, start = place // edge, place % edge
        total = jnp.zeros((tall, LANES), jnp.float32)
        for k in range(cap):
            total = total + prods[k, :, start : start + LANES] * picks[s][k]
        block, start = place // share, place % share
        out_part[block, :, start : start + LANES] = total
        if (place + LANES) % (2 * share) == 0:
            pair_copy(block // 2).start()

    low_half = lax.broadcasted_iota(jnp.int32, (tall, share), 0) >= dim + PAD // 2
    copies = []
    for off in range(1, layers):
        other = lax.rem(layer + off, layers)
        pair_copy(other).wait()
        total = out_part[2 * other + core] + pair_recv[other]
        rest = total - total.astype(jnp.bfloat16).astype(jnp.float32)
        out_send[off - 1] = jnp.where(low_half, rest, total).astype(jnp.bfloat16)
        copy = pltpu.make_async_remote_copy(
            src_ref=out_send.at[off - 1],
            dst_ref=out_recv.at[off - 1],
            send_sem=out_send_sem.at[off - 1],
            recv_sem=out_recv_sem.at[off - 1],
            device_id={"tgt": 2 * other + core},
            device_id_type=MESH,
        )
        copy.start()
        copies.append(copy)
    pair_copy(layer).wait()
    total = out_part[2 * layer + core] + pair_recv[layer]
    total = jnp.where(low_half, 0.0, total)
    for off, copy in enumerate(copies):
        copy.wait()
        total = total + out_recv[off].astype(jnp.float32)
    mass = total[dim : dim + 1] + total[dim + PAD // 2 : dim + PAD // 2 + 1]
    out_ref[...] = total[:dim] / mass


def local(n_src, n_tgt, tile_cost, tile_pairs, tile_counts, src_mass, tgt_mass, targets_t):
    cap, edge = tile_cost.shape[0], tile_cost.shape[1]
    src_tiles, tgt_tiles = src_mass.shape[0] // edge, tgt_mass.shape[0] // edge
    dim = targets_t.shape[0]
    share = src_mass.shape[0] // n_tgt
    tall = dim + PAD
    f32, bf16 = jnp.float32, jnp.bfloat16
    dma = pltpu.SemaphoreType.DMA
    smem = pl.BlockSpec(memory_space=pltpu.SMEM)
    vmem = pl.BlockSpec(memory_space=pltpu.VMEM)
    hbm = pl.BlockSpec(memory_space=pl.ANY)
    return pl.pallas_call(
        functools.partial(kernel, n_src, n_tgt),
        out_shape=jax.ShapeDtypeStruct((dim, share), f32),
        in_specs=[smem, smem, hbm, vmem, vmem, hbm],
        out_specs=vmem,
        scratch_shapes=[
            pltpu.VMEM((cap, edge, edge), bf16),
            pltpu.VMEM((cap, edge, edge), f32),
            pltpu.VMEM((2, edge, LANES), f32),
            pltpu.VMEM((tgt_tiles, tall, edge), bf16),
            pltpu.VMEM((cap, tall, edge), f32),
            pltpu.VMEM((edge, LANES), f32),
            pltpu.VMEM((PAD, edge), f32),
            pltpu.VMEM((LANES, edge), f32),
            pltpu.VMEM((src_tiles, edge, LANES), f32),
            pltpu.VMEM((cap, 8, edge), f32),
            pltpu.VMEM((cap, 8, edge), f32),
            pltpu.VMEM((cap, 8, edge), f32),
            pltpu.VMEM((tgt_tiles, 8, edge), f32),
            pltpu.VMEM((src_tiles, edge), f32),
            pltpu.VMEM((tgt_tiles, edge), f32),
            pltpu.VMEM((n_tgt, src_tiles, edge), f32),
            pltpu.VMEM((n_tgt, src_tiles, edge), f32),
            pltpu.VMEM((n_src, tgt_tiles, edge), f32),
            pltpu.VMEM((n_src, tgt_tiles, edge), f32),
            pltpu.VMEM((n_tgt, tall, share), f32),
            pltpu.VMEM((n_tgt // 2, tall, share), f32),
            pltpu.VMEM((n_tgt // 2 - 1, tall, share), bf16),
            pltpu.VMEM((n_tgt // 2 - 1, tall, share), bf16),
            dma((cap,)),
            dma((tgt_tiles,)),
            dma((n_tgt - 1,)),
            dma((n_tgt - 1,)),
            dma((n_tgt - 1,)),
            dma((n_tgt - 1,)),
            dma((n_src - 1,)),
            dma((n_src - 1,)),
            dma((n_src - 1,)),
            dma((n_src - 1,)),
            dma((n_tgt // 2,)),
            dma((n_tgt // 2,)),
            dma((n_tgt // 2 - 1,)),
            dma((n_tgt // 2 - 1,)),
        ],
        compiler_params=pltpu.CompilerParams(
            collective_id=0, has_side_effects=True, vmem_limit_bytes=56 * 1024 * 1024
        ),
    )(
        tile_pairs.T,
        tile_counts,
        tile_cost,
        src_mass,
        tgt_mass,
        targets_t,
    )


def solution(mesh):
    return jax.shard_map(
        functools.partial(local, mesh.shape["src"], mesh.shape["tgt"]),
        mesh=mesh,
        in_specs=(
            P(("src", "tgt"), None, None),
            P(("src", "tgt"), None),
            P(("src", "tgt")),
            P("src"),
            P("tgt"),
            P(None, "tgt"),
        ),
        out_specs=P(None, ("src", "tgt")),
        check_vma=False,
    )
```

```python
import functools

import jax
import jax.numpy as jnp
from jax import lax
from jax.experimental import pallas as pl
from jax.experimental.pallas import tpu as pltpu
from jax.sharding import PartitionSpec as P

MESH = pl.DeviceIdType.MESH
inverse_eps = 50.0 * 1.4426950408889634
negative_floor = -1e30
ROWS = 64
LANES = 128
PAD = 16


def logsumexp0(parts):
    top = jnp.max(parts, axis=0)
    return top + jnp.log2(jnp.sum(jnp.exp2(parts - top[None]), axis=0))


def kernel(
    n_src,
    n_tgt,
    pairs_ref,
    count_ref,
    cost_hbm,
    src_mass_flat,
    tgt_mass_flat,
    targets_hbm,
    out_ref,
    cost,
    q,
    low,
    tgts,
    prods,
    slot_cols,
    slot_rows,
    pad_rows,
    row_pot,
    col_stab,
    col_sum,
    col_fac,
    tgt_pot,
    src_mass_ref,
    tgt_mass_ref,
    row_buf1,
    row_buf2,
    col_buf1,
    col_buf2,
    out_part,
    pair_recv,
    out_send,
    out_recv,
    mass_send,
    mass_recv,
    cost_sem,
    tgts_sem,
    row_send1,
    row_recv1,
    row_send2,
    row_recv2,
    col_send1,
    col_recv1,
    col_send2,
    col_recv2,
    pair_send_sem,
    pair_recv_sem,
    out_send_sem,
    out_recv_sem,
):
    cap, edge = cost.shape[0], cost.shape[1]
    src_tiles, tgt_tiles = src_mass_ref.shape[0], tgt_mass_ref.shape[0]
    dim = targets_hbm.shape[0]
    my_src, my_tgt = lax.axis_index("src"), lax.axis_index("tgt")
    chunks = edge // ROWS

    for k in range(cap):
        pltpu.make_async_copy(cost_hbm.at[k], cost.at[k], cost_sem.at[k]).start()
    for t in range(tgt_tiles):
        pltpu.make_async_copy(
            targets_hbm.at[:, pl.ds(t * edge, edge)], tgts.at[t, pl.ds(0, dim)], tgts_sem.at[t]
        ).start()

    barrier = pltpu.get_barrier_semaphore()
    for off in range(1, n_tgt):
        pl.semaphore_signal(
            barrier, inc=1, device_id={"tgt": lax.rem(my_tgt + off, n_tgt)}, device_id_type=MESH
        )
    for off in range(1, n_src):
        pl.semaphore_signal(
            barrier, inc=1, device_id={"src": lax.rem(my_src + off, n_src)}, device_id_type=MESH
        )

    pad_rows[...] = jnp.zeros_like(pad_rows)
    slot_cols[...] = jnp.zeros_like(slot_cols)
    tgts[:, dim:, :] = jnp.ones((tgt_tiles, PAD, edge), jnp.bfloat16)

    for s in range(src_tiles):
        src_mass_ref[s : s + 1, :] = src_mass_flat[s * edge : (s + 1) * edge].reshape(1, edge)
    for t in range(tgt_tiles):
        tgt_mass_ref[t : t + 1, :] = tgt_mass_flat[t * edge : (t + 1) * edge].reshape(1, edge)

    count = count_ref[0]
    src_of = [lax.rem(pairs_ref[0, k], src_tiles) for k in range(cap)]
    tgt_of = [lax.rem(pairs_ref[1, k], tgt_tiles) for k in range(cap)]
    src_id = [jnp.where(k < count, src_of[k], -1) for k in range(cap)]
    tgt_id = [jnp.where(k < count, tgt_of[k], -1) for k in range(cap)]
    src_rows = lax.broadcasted_iota(jnp.int32, (src_tiles, edge), 0)
    tgt_rows = lax.broadcasted_iota(jnp.int32, (tgt_tiles, edge), 0)
    lane = lax.broadcasted_iota(jnp.int32, (ROWS, LANES), 1)

    def wide(block):
        return jnp.concatenate([block] * (edge // LANES), axis=1)

    def put_column(k, c, value):
        rows = slice(c * ROWS, (c + 1) * ROWS)
        slot_cols[rows, :] = jnp.where(lane == k, value, slot_cols[rows, :])

    def slots_as_rows():
        slot_rows[...] = slot_cols[...].T[:PAD]

    def spread_rows(values):
        pad_rows[0:src_tiles, :] = values
        columns = pad_rows[...].T
        for s in range(src_tiles):
            row_pot[s] = jnp.broadcast_to(columns[:, s : s + 1], (edge, LANES))

    def exchange(buf, axis, me, n, send_sem, recv_sem):
        copies = []
        for off in range(1, n):
            copy = pltpu.make_async_remote_copy(
                src_ref=buf.at[0],
                dst_ref=buf.at[off],
                send_sem=send_sem.at[off - 1],
                recv_sem=recv_sem.at[off - 1],
                device_id={axis: lax.rem(me + off, n)},
                device_id_type=MESH,
            )
            copy.start()
            copies.append(copy)
        for copy in copies:
            copy.wait()

    def merge_logs(parts, ids, rows):
        top = jnp.full(rows.shape, negative_floor, jnp.float32)
        for part, tile in zip(parts, ids):
            top = jnp.maximum(top, jnp.where(rows == tile, part, negative_floor))
        total = jnp.zeros(rows.shape, jnp.float32)
        for part, tile in zip(parts, ids):
            total = total + jnp.where(rows == tile, jnp.exp2(part - top), 0.0)
        return jnp.where(total > 0.0, top + jnp.log2(total), negative_floor)

    def merge_sums(parts, ids, rows):
        total = jnp.zeros(rows.shape, jnp.float32)
        for part, tile in zip(parts, ids):
            total = total + jnp.where(rows == tile, part, 0.0)
        return total

    def halves(combine, block):
        parts = [block[:, at : at + LANES] for at in range(0, edge, LANES)]
        return functools.reduce(combine, parts)

    def in_pairs(step):
        def both(i, carry):
            step(2 * i)
            step(2 * i + 1)
            return carry

        lax.fori_loop(0, cap // 2, both, 0)

    def row_first(i, carry):
        for u in range(2):
            k = 2 * i + u
            pltpu.make_async_copy(cost_hbm.at[k], cost.at[k], cost_sem.at[k]).wait()
            for c in range(chunks):
                rows = slice(c * ROWS, (c + 1) * ROWS)
                tile = cost[k, rows, :].astype(jnp.float32) * inverse_eps
                q[k, rows, :] = tile
                least = jnp.min(halves(jnp.minimum, tile), axis=1, keepdims=True)
                low[u, rows, :] = jnp.broadcast_to(least, (ROWS, LANES))
        for u in range(2):
            k = 2 * i + u
            for c in range(chunks):
                rows = slice(c * ROWS, (c + 1) * ROWS)
                value = jnp.exp2(wide(low[u, rows, :]) - q[k, rows, :])
                total = jnp.sum(halves(jnp.add, value), axis=1, keepdims=True)
                put_column(k, c, jnp.log2(total) - low[u, rows, :])
        return carry

    lax.fori_loop(0, cap // 2, row_first, 0)
    slots_as_rows()
    row_buf1[0] = merge_logs([slot_rows[k : k + 1, :] for k in range(cap)], src_id, src_rows)
    pl.semaphore_wait(barrier, n_tgt - 1 + n_src - 1)
    exchange(row_buf1, "tgt", my_tgt, n_tgt, row_send1, row_recv1)
    spread_rows(jnp.log2(src_mass_ref[...]) - logsumexp0(row_buf1[...]))

    def col_first(i, carry):
        tops = []
        for u in range(2):
            k = 2 * i + u
            s = lax.rem(pairs_ref[0, k], src_tiles)
            top = jnp.full((8, edge), negative_floor, jnp.float32)
            for c in range(chunks):
                rows = slice(c * ROWS, (c + 1) * ROWS)
                score = wide(row_pot[s, rows, :]) - q[k, rows, :]
                top = jnp.maximum(top, jnp.max(score.reshape(ROWS // 8, 8, edge), axis=0))
            tops.append(jnp.broadcast_to(jnp.max(top, axis=0, keepdims=True), (8, edge)))
        for u in range(2):
            k = 2 * i + u
            s = lax.rem(pairs_ref[0, k], src_tiles)
            total = jnp.zeros((8, edge), jnp.float32)
            for c in range(chunks):
                rows = slice(c * ROWS, (c + 1) * ROWS)
                score = (wide(row_pot[s, rows, :]) - q[k, rows, :]).reshape(ROWS // 8, 8, edge)
                value = jnp.exp2(score - tops[u][None])
                q[k, rows, :] = value.reshape(ROWS, edge)
                total = total + jnp.sum(value, axis=0)
            col_stab[k] = tops[u]
            col_sum[k] = jnp.broadcast_to(jnp.sum(total, axis=0, keepdims=True), (8, edge))
        return carry

    lax.fori_loop(0, cap // 2, col_first, 0)
    col_buf1[0] = merge_logs(
        [col_stab[k, 0:1, :] + jnp.log2(col_sum[k, 0:1, :]) for k in range(cap)], tgt_id, tgt_rows
    )
    exchange(col_buf1, "src", my_src, n_src, col_send1, col_recv1)
    potential = jnp.log2(tgt_mass_ref[...]) - logsumexp0(col_buf1[...])
    for t in range(tgt_tiles):
        tgt_pot[t] = jnp.broadcast_to(potential[t : t + 1, :], (8, edge))

    def row_second(k):
        t = lax.rem(pairs_ref[1, k], tgt_tiles)
        alive = jnp.full((8, edge), k, jnp.int32) < count
        factor = jnp.where(alive, jnp.exp2(tgt_pot[t] + col_stab[k]), 0.0)
        col_fac[k] = factor
        for c in range(chunks):
            rows = slice(c * ROWS, (c + 1) * ROWS)
            value = q[k, rows, :].reshape(ROWS // 8, 8, edge) * factor[None]
            total = halves(jnp.add, value.reshape(ROWS, edge))
            put_column(k, c, jnp.sum(total, axis=1, keepdims=True))

    in_pairs(row_second)
    slots_as_rows()
    row_buf2[0] = merge_sums([slot_rows[k : k + 1, :] for k in range(cap)], src_id, src_rows)
    exchange(row_buf2, "tgt", my_tgt, n_tgt, row_send2, row_recv2)
    spread_rows(src_mass_ref[...] / jnp.sum(row_buf2[...], axis=0))

    def col_second(k):
        s = lax.rem(pairs_ref[0, k], src_tiles)
        total = jnp.zeros((8, edge), jnp.float32)
        for c in range(chunks):
            rows = slice(c * ROWS, (c + 1) * ROWS)
            value = q[k, rows, :] * wide(row_pot[s, rows, :])
            q[k, rows, :] = value
            total = total + jnp.sum(value.reshape(ROWS // 8, 8, edge), axis=0)
        col_sum[k] = jnp.broadcast_to(jnp.sum(total, axis=0, keepdims=True), (8, edge)) * col_fac[k]

    in_pairs(col_second)
    col_buf2[0] = merge_sums([col_sum[k, 0:1, :] for k in range(cap)], tgt_id, tgt_rows)
    exchange(col_buf2, "src", my_src, n_src, col_send2, col_recv2)
    potential = tgt_mass_ref[...] / jnp.sum(col_buf2[...], axis=0)
    for t in range(tgt_tiles):
        tgt_pot[t] = jnp.broadcast_to(potential[t : t + 1, :], (8, edge))

    for t in range(tgt_tiles):
        pltpu.make_async_copy(
            targets_hbm.at[:, pl.ds(t * edge, edge)], tgts.at[t, pl.ds(0, dim)], tgts_sem.at[t]
        ).wait()

    def map_slot(k):
        t = lax.rem(pairs_ref[1, k], tgt_tiles)
        factor = tgt_pot[t] * col_fac[k]
        left = tgts[t]
        for h in range(edge // 256):
            parts = []
            for c in range(256 // ROWS):
                rows = slice(h * 256 + c * ROWS, h * 256 + (c + 1) * ROWS)
                value = q[k, rows, :].reshape(ROWS // 8, 8, edge)
                parts.append((value * factor[None]).reshape(ROWS, edge).astype(jnp.bfloat16))
            prods[k, :, h * 256 : (h + 1) * 256] = lax.dot_general(
                left,
                jnp.concatenate(parts, axis=0),
                (((1,), (1,)), ((), ())),
                preferred_element_type=jnp.float32,
            )

    in_pairs(map_slot)

    share = out_ref.shape[1]
    tall = dim + PAD
    core, layer, layers = lax.rem(my_tgt, 2), my_tgt // 2, n_tgt // 2

    def pair_copy(j):
        return pltpu.make_async_remote_copy(
            src_ref=out_part.at[2 * j + 1 - core],
            dst_ref=pair_recv.at[j],
            send_sem=pair_send_sem.at[j],
            recv_sem=pair_recv_sem.at[j],
            device_id={"tgt": my_tgt + 1 - 2 * core},
            device_id_type=MESH,
        )

    picks = [
        [jnp.where(src_id[k] == s, 1.0, 0.0) for k in range(cap)] for s in range(src_tiles)
    ]
    for place in range(0, src_tiles * edge, LANES):
        s, start = place // edge, place % edge
        total = jnp.zeros((tall, LANES), jnp.float32)
        for k in range(cap):
            total = total + prods[k, :, start : start + LANES] * picks[s][k]
        block, start = place // share, place % share
        out_part[block, :, start : start + LANES] = total
        if (place + LANES) % (2 * share) == 0:
            pair_copy(block // 2).start()

    copies = []
    for off in range(1, layers):
        other = lax.rem(layer + off, layers)
        pair_copy(other).wait()
        block = 2 * other + core
        out_send[off - 1] = (out_part[block, :dim] + pair_recv[other, :dim]).astype(jnp.bfloat16)
        mass_send[off - 1] = out_part[block, dim : dim + 1] + pair_recv[other, dim : dim + 1]
        for kind, (sent, landed) in enumerate(((out_send, out_recv), (mass_send, mass_recv))):
            copy = pltpu.make_async_remote_copy(
                src_ref=sent.at[off - 1],
                dst_ref=landed.at[off - 1],
                send_sem=out_send_sem.at[kind, off - 1],
                recv_sem=out_recv_sem.at[kind, off - 1],
                device_id={"tgt": block},
                device_id_type=MESH,
            )
            copy.start()
            copies.append(copy)
    pair_copy(layer).wait()
    block = 2 * layer + core
    total = out_part[block, :dim] + pair_recv[layer, :dim]
    mass = out_part[block, dim : dim + 1] + pair_recv[layer, dim : dim + 1]
    for off in range(layers - 1):
        copies[2 * off].wait()
        copies[2 * off + 1].wait()
        total = total + out_recv[off].astype(jnp.float32)
        mass = mass + mass_recv[off]
    out_ref[...] = total / mass


def local(n_src, n_tgt, tile_cost, tile_pairs, tile_counts, src_mass, tgt_mass, targets_t):
    cap, edge = tile_cost.shape[0], tile_cost.shape[1]
    src_tiles, tgt_tiles = src_mass.shape[0] // edge, tgt_mass.shape[0] // edge
    dim = targets_t.shape[0]
    share = src_mass.shape[0] // n_tgt
    tall = dim + PAD
    f32, bf16 = jnp.float32, jnp.bfloat16
    dma = pltpu.SemaphoreType.DMA
    smem = pl.BlockSpec(memory_space=pltpu.SMEM)
    vmem = pl.BlockSpec(memory_space=pltpu.VMEM)
    hbm = pl.BlockSpec(memory_space=pl.ANY)
    return pl.pallas_call(
        functools.partial(kernel, n_src, n_tgt),
        out_shape=jax.ShapeDtypeStruct((dim, share), f32),
        in_specs=[smem, smem, hbm, vmem, vmem, hbm],
        out_specs=vmem,
        scratch_shapes=[
            pltpu.VMEM((cap, edge, edge), bf16),
            pltpu.VMEM((cap, edge, edge), f32),
            pltpu.VMEM((2, edge, LANES), f32),
            pltpu.VMEM((tgt_tiles, tall, edge), bf16),
            pltpu.VMEM((cap, tall, edge), f32),
            pltpu.VMEM((edge, LANES), f32),
            pltpu.VMEM((PAD, edge), f32),
            pltpu.VMEM((LANES, edge), f32),
            pltpu.VMEM((src_tiles, edge, LANES), f32),
            pltpu.VMEM((cap, 8, edge), f32),
            pltpu.VMEM((cap, 8, edge), f32),
            pltpu.VMEM((cap, 8, edge), f32),
            pltpu.VMEM((tgt_tiles, 8, edge), f32),
            pltpu.VMEM((src_tiles, edge), f32),
            pltpu.VMEM((tgt_tiles, edge), f32),
            pltpu.VMEM((n_tgt, src_tiles, edge), f32),
            pltpu.VMEM((n_tgt, src_tiles, edge), f32),
            pltpu.VMEM((n_src, tgt_tiles, edge), f32),
            pltpu.VMEM((n_src, tgt_tiles, edge), f32),
            pltpu.VMEM((n_tgt, tall, share), f32),
            pltpu.VMEM((n_tgt // 2, tall, share), f32),
            pltpu.VMEM((n_tgt // 2 - 1, dim, share), bf16),
            pltpu.VMEM((n_tgt // 2 - 1, dim, share), bf16),
            pltpu.VMEM((n_tgt // 2 - 1, 1, share), f32),
            pltpu.VMEM((n_tgt // 2 - 1, 1, share), f32),
            dma((cap,)),
            dma((tgt_tiles,)),
            dma((n_tgt - 1,)),
            dma((n_tgt - 1,)),
            dma((n_tgt - 1,)),
            dma((n_tgt - 1,)),
            dma((n_src - 1,)),
            dma((n_src - 1,)),
            dma((n_src - 1,)),
            dma((n_src - 1,)),
            dma((n_tgt // 2,)),
            dma((n_tgt // 2,)),
            dma((2, n_tgt // 2 - 1)),
            dma((2, n_tgt // 2 - 1)),
        ],
        compiler_params=pltpu.CompilerParams(
            collective_id=0, has_side_effects=True, vmem_limit_bytes=56 * 1024 * 1024
        ),
    )(
        tile_pairs.T,
        tile_counts,
        tile_cost,
        src_mass,
        tgt_mass,
        targets_t,
    )


def solution(mesh):
    return jax.shard_map(
        functools.partial(local, mesh.shape["src"], mesh.shape["tgt"]),
        mesh=mesh,
        in_specs=(
            P(("src", "tgt"), None, None),
            P(("src", "tgt"), None),
            P(("src", "tgt")),
            P("src"),
            P("tgt"),
            P(None, "tgt"),
        ),
        out_specs=P(None, ("src", "tgt")),
        check_vma=False,
    )
```

```python
import functools

import jax
import jax.numpy as jnp
from jax import lax
from jax.experimental import pallas as pl
from jax.experimental.pallas import tpu as pltpu
from jax.sharding import PartitionSpec as P

MESH = pl.DeviceIdType.MESH
inverse_eps = 50.0 * 1.4426950408889634
negative_floor = -1e30
ROWS = 64
LANES = 128
PAD = 16


def logsumexp0(parts):
    top = jnp.max(parts, axis=0)
    return top + jnp.log2(jnp.sum(jnp.exp2(parts - top[None]), axis=0))


def kernel(
    n_src,
    n_tgt,
    pairs_ref,
    count_ref,
    cost_hbm,
    src_mass_flat,
    tgt_mass_flat,
    targets_hbm,
    out_ref,
    cost,
    q,
    low,
    tgts,
    prods,
    slot_cols,
    slot_rows,
    pad_rows,
    row_pot,
    col_stab,
    col_sum,
    col_fac,
    tgt_pot,
    src_mass_ref,
    tgt_mass_ref,
    row_buf1,
    row_buf2,
    col_buf1,
    col_buf2,
    out_part,
    pair_recv,
    out_send,
    out_recv,
    mass_send,
    mass_recv,
    cost_sem,
    tgts_sem,
    row_send1,
    row_recv1,
    row_send2,
    row_recv2,
    col_send1,
    col_recv1,
    col_send2,
    col_recv2,
    pair_send_sem,
    pair_recv_sem,
    out_send_sem,
    out_recv_sem,
):
    cap, edge = cost.shape[0], cost.shape[1]
    src_tiles, tgt_tiles = src_mass_ref.shape[0], tgt_mass_ref.shape[0]
    dim = targets_hbm.shape[0]
    my_src, my_tgt = lax.axis_index("src"), lax.axis_index("tgt")
    chunks = edge // ROWS

    for k in range(cap):
        pltpu.make_async_copy(cost_hbm.at[k], cost.at[k], cost_sem.at[k]).start()
    for t in range(tgt_tiles):
        pltpu.make_async_copy(
            targets_hbm.at[:, pl.ds(t * edge, edge)], tgts.at[t, pl.ds(0, dim)], tgts_sem.at[t]
        ).start()

    barrier = pltpu.get_barrier_semaphore()
    for off in range(1, n_tgt):
        pl.semaphore_signal(
            barrier, inc=1, device_id={"tgt": lax.rem(my_tgt + off, n_tgt)}, device_id_type=MESH
        )
    for off in range(1, n_src):
        pl.semaphore_signal(
            barrier, inc=1, device_id={"src": lax.rem(my_src + off, n_src)}, device_id_type=MESH
        )

    pad_rows[...] = jnp.zeros_like(pad_rows)
    slot_cols[...] = jnp.zeros_like(slot_cols)
    tgts[:, dim:, :] = jnp.ones((tgt_tiles, PAD, edge), jnp.bfloat16)

    for s in range(src_tiles):
        src_mass_ref[s : s + 1, :] = src_mass_flat[s * edge : (s + 1) * edge].reshape(1, edge)
    for t in range(tgt_tiles):
        tgt_mass_ref[t : t + 1, :] = tgt_mass_flat[t * edge : (t + 1) * edge].reshape(1, edge)

    count = count_ref[0]
    src_of = [lax.rem(pairs_ref[0, k], src_tiles) for k in range(cap)]
    tgt_of = [lax.rem(pairs_ref[1, k], tgt_tiles) for k in range(cap)]
    src_id = [jnp.where(k < count, src_of[k], -1) for k in range(cap)]
    tgt_id = [jnp.where(k < count, tgt_of[k], -1) for k in range(cap)]
    src_rows = lax.broadcasted_iota(jnp.int32, (src_tiles, edge), 0)
    tgt_rows = lax.broadcasted_iota(jnp.int32, (tgt_tiles, edge), 0)
    lane = lax.broadcasted_iota(jnp.int32, (ROWS, LANES), 1)

    def wide(block):
        return jnp.concatenate([block] * (edge // LANES), axis=1)

    def put_column(k, c, value):
        rows = slice(c * ROWS, (c + 1) * ROWS)
        slot_cols[rows, :] = jnp.where(lane == k, value, slot_cols[rows, :])

    def slots_as_rows():
        slot_rows[...] = slot_cols[...].T[:PAD]

    def spread_rows(values):
        pad_rows[0:src_tiles, :] = values
        columns = pad_rows[...].T
        for s in range(src_tiles):
            row_pot[s] = jnp.broadcast_to(columns[:, s : s + 1], (edge, LANES))

    def exchange(buf, axis, me, n, send_sem, recv_sem):
        copies = []
        for off in range(1, n):
            copy = pltpu.make_async_remote_copy(
                src_ref=buf.at[0],
                dst_ref=buf.at[off],
                send_sem=send_sem.at[off - 1],
                recv_sem=recv_sem.at[off - 1],
                device_id={axis: lax.rem(me + off, n)},
                device_id_type=MESH,
            )
            copy.start()
            copies.append(copy)
        for copy in copies:
            copy.wait()

    def merge_logs(parts, ids, rows):
        top = jnp.full(rows.shape, negative_floor, jnp.float32)
        for part, tile in zip(parts, ids):
            top = jnp.maximum(top, jnp.where(rows == tile, part, negative_floor))
        total = jnp.zeros(rows.shape, jnp.float32)
        for part, tile in zip(parts, ids):
            total = total + jnp.where(rows == tile, jnp.exp2(part - top), 0.0)
        return jnp.where(total > 0.0, top + jnp.log2(total), negative_floor)

    def merge_sums(parts, ids, rows):
        total = jnp.zeros(rows.shape, jnp.float32)
        for part, tile in zip(parts, ids):
            total = total + jnp.where(rows == tile, part, 0.0)
        return total

    def halves(combine, block):
        parts = [block[:, at : at + LANES] for at in range(0, edge, LANES)]
        return functools.reduce(combine, parts)

    def in_pairs(step):
        def both(i, carry):
            step(2 * i)
            step(2 * i + 1)
            return carry

        lax.fori_loop(0, cap // 2, both, 0)

    def row_first(i, carry):
        for u in range(2):
            k = 2 * i + u
            pltpu.make_async_copy(cost_hbm.at[k], cost.at[k], cost_sem.at[k]).wait()
            for c in range(chunks):
                rows = slice(c * ROWS, (c + 1) * ROWS)
                tile = cost[k, rows, :].astype(jnp.float32) * inverse_eps
                q[k, rows, :] = tile
                least = jnp.min(halves(jnp.minimum, tile), axis=1, keepdims=True)
                low[u, rows, :] = jnp.broadcast_to(least, (ROWS, LANES))
        for u in range(2):
            k = 2 * i + u
            for c in range(chunks):
                rows = slice(c * ROWS, (c + 1) * ROWS)
                value = jnp.exp2(wide(low[u, rows, :]) - q[k, rows, :])
                total = jnp.sum(halves(jnp.add, value), axis=1, keepdims=True)
                put_column(k, c, jnp.log2(total) - low[u, rows, :])
        return carry

    lax.fori_loop(0, cap // 2, row_first, 0)
    slots_as_rows()
    row_buf1[0] = merge_logs([slot_rows[k : k + 1, :] for k in range(cap)], src_id, src_rows)
    pl.semaphore_wait(barrier, n_tgt - 1 + n_src - 1)
    exchange(row_buf1, "tgt", my_tgt, n_tgt, row_send1, row_recv1)
    spread_rows(jnp.log2(src_mass_ref[...]) - logsumexp0(row_buf1[...]))

    def col_first(i, carry):
        tops = []
        for u in range(2):
            k = 2 * i + u
            s = lax.rem(pairs_ref[0, k], src_tiles)
            top = jnp.full((8, edge), negative_floor, jnp.float32)
            for c in range(chunks):
                rows = slice(c * ROWS, (c + 1) * ROWS)
                score = wide(row_pot[s, rows, :]) - q[k, rows, :]
                top = jnp.maximum(top, jnp.max(score.reshape(ROWS // 8, 8, edge), axis=0))
            tops.append(jnp.broadcast_to(jnp.max(top, axis=0, keepdims=True), (8, edge)))
        for u in range(2):
            k = 2 * i + u
            s = lax.rem(pairs_ref[0, k], src_tiles)
            total = jnp.zeros((8, edge), jnp.float32)
            for c in range(chunks):
                rows = slice(c * ROWS, (c + 1) * ROWS)
                score = (wide(row_pot[s, rows, :]) - q[k, rows, :]).reshape(ROWS // 8, 8, edge)
                value = jnp.exp2(score - tops[u][None])
                q[k, rows, :] = value.reshape(ROWS, edge)
                total = total + jnp.sum(value, axis=0)
            col_stab[k] = tops[u]
            col_sum[k] = jnp.broadcast_to(jnp.sum(total, axis=0, keepdims=True), (8, edge))
        return carry

    lax.fori_loop(0, cap // 2, col_first, 0)
    col_buf1[0] = merge_logs(
        [col_stab[k, 0:1, :] + jnp.log2(col_sum[k, 0:1, :]) for k in range(cap)], tgt_id, tgt_rows
    )
    exchange(col_buf1, "src", my_src, n_src, col_send1, col_recv1)
    potential = jnp.log2(tgt_mass_ref[...]) - logsumexp0(col_buf1[...])
    for t in range(tgt_tiles):
        tgt_pot[t] = jnp.broadcast_to(potential[t : t + 1, :], (8, edge))

    def row_second(k):
        t = lax.rem(pairs_ref[1, k], tgt_tiles)
        alive = jnp.full((8, edge), k, jnp.int32) < count
        factor = jnp.where(alive, jnp.exp2(tgt_pot[t] + col_stab[k]), 0.0)
        col_fac[k] = factor
        for c in range(chunks):
            rows = slice(c * ROWS, (c + 1) * ROWS)
            value = q[k, rows, :].reshape(ROWS // 8, 8, edge) * factor[None]
            total = halves(jnp.add, value.reshape(ROWS, edge))
            put_column(k, c, jnp.sum(total, axis=1, keepdims=True))

    in_pairs(row_second)
    slots_as_rows()
    row_buf2[0] = merge_sums([slot_rows[k : k + 1, :] for k in range(cap)], src_id, src_rows)
    exchange(row_buf2, "tgt", my_tgt, n_tgt, row_send2, row_recv2)
    spread_rows(src_mass_ref[...] / jnp.sum(row_buf2[...], axis=0))

    def col_second(k):
        s = lax.rem(pairs_ref[0, k], src_tiles)
        total = jnp.zeros((8, edge), jnp.float32)
        for c in range(chunks):
            rows = slice(c * ROWS, (c + 1) * ROWS)
            value = q[k, rows, :] * wide(row_pot[s, rows, :])
            q[k, rows, :] = value
            total = total + jnp.sum(value.reshape(ROWS // 8, 8, edge), axis=0)
        col_sum[k] = jnp.broadcast_to(jnp.sum(total, axis=0, keepdims=True), (8, edge)) * col_fac[k]

    in_pairs(col_second)
    col_buf2[0] = merge_sums([col_sum[k, 0:1, :] for k in range(cap)], tgt_id, tgt_rows)
    exchange(col_buf2, "src", my_src, n_src, col_send2, col_recv2)
    potential = tgt_mass_ref[...] / jnp.sum(col_buf2[...], axis=0)
    for t in range(tgt_tiles):
        tgt_pot[t] = jnp.broadcast_to(potential[t : t + 1, :], (8, edge))

    for t in range(tgt_tiles):
        pltpu.make_async_copy(
            targets_hbm.at[:, pl.ds(t * edge, edge)], tgts.at[t, pl.ds(0, dim)], tgts_sem.at[t]
        ).wait()

    def map_slot(k):
        t = lax.rem(pairs_ref[1, k], tgt_tiles)
        factor = tgt_pot[t] * col_fac[k]
        left = tgts[t]
        for h in range(edge // 256):
            parts = []
            for c in range(256 // ROWS):
                rows = slice(h * 256 + c * ROWS, h * 256 + (c + 1) * ROWS)
                value = q[k, rows, :].reshape(ROWS // 8, 8, edge)
                parts.append((value * factor[None]).reshape(ROWS, edge).astype(jnp.bfloat16))
            prods[k, :, h * 256 : (h + 1) * 256] = lax.dot_general(
                left,
                jnp.concatenate(parts, axis=0),
                (((1,), (1,)), ((), ())),
                preferred_element_type=jnp.float32,
            )

    in_pairs(map_slot)

    share = out_ref.shape[1]
    tall = dim + PAD
    core, layer, layers = lax.rem(my_tgt, 2), my_tgt // 2, n_tgt // 2

    def pair_copy(j):
        return pltpu.make_async_remote_copy(
            src_ref=out_part.at[2 * j + 1 - core],
            dst_ref=pair_recv.at[j],
            send_sem=pair_send_sem.at[j],
            recv_sem=pair_recv_sem.at[j],
            device_id={"tgt": my_tgt + 1 - 2 * core},
            device_id_type=MESH,
        )

    def layer_copies(other, slot):
        return [
            pltpu.make_async_remote_copy(
                src_ref=sent.at[slot],
                dst_ref=landed.at[slot],
                send_sem=out_send_sem.at[kind, slot],
                recv_sem=out_recv_sem.at[kind, slot],
                device_id={"tgt": 2 * other + core},
                device_id_type=MESH,
            )
            for kind, (sent, landed) in enumerate(((out_send, out_recv), (mass_send, mass_recv)))
        ]

    def ship(j):
        @pl.when(layer != j)
        def _():
            slot = lax.rem(j - layer + layers, layers) - 1
            block = 2 * j + core
            pair_copy(j).wait_recv()
            out_send[slot] = (out_part[block, :dim] + pair_recv[j, :dim]).astype(jnp.bfloat16)
            mass_send[slot] = out_part[block, dim : dim + 1] + pair_recv[j, dim : dim + 1]
            for copy in layer_copies(j, slot):
                copy.start()

    picks = [
        [jnp.where(src_id[k] == s, 1.0, 0.0) for k in range(cap)] for s in range(src_tiles)
    ]
    for place in range(0, src_tiles * edge, LANES):
        s, start = place // edge, place % edge
        total = jnp.zeros((tall, LANES), jnp.float32)
        for k in range(cap):
            total = total + prods[k, :, start : start + LANES] * picks[s][k]
        block, start = place // share, place % share
        out_part[block, :, start : start + LANES] = total
        if (place + LANES) % (2 * share) == 0:
            pair_copy(block // 2).start()
            if block > 2:
                ship(block // 2 - 1)
    ship(layers - 1)

    for off in range(1, layers):
        pair_copy(lax.rem(layer + off, layers)).wait_send()
    pair_copy(layer).wait()
    block = 2 * layer + core
    total = out_part[block, :dim] + pair_recv[layer, :dim]
    mass = out_part[block, dim : dim + 1] + pair_recv[layer, dim : dim + 1]
    for off in range(layers - 1):
        for copy in layer_copies(lax.rem(layer + off + 1, layers), off):
            copy.wait()
        total = total + out_recv[off].astype(jnp.float32)
        mass = mass + mass_recv[off]
    out_ref[...] = total / mass


def local(n_src, n_tgt, tile_cost, tile_pairs, tile_counts, src_mass, tgt_mass, targets_t):
    cap, edge = tile_cost.shape[0], tile_cost.shape[1]
    src_tiles, tgt_tiles = src_mass.shape[0] // edge, tgt_mass.shape[0] // edge
    dim = targets_t.shape[0]
    share = src_mass.shape[0] // n_tgt
    tall = dim + PAD
    f32, bf16 = jnp.float32, jnp.bfloat16
    dma = pltpu.SemaphoreType.DMA
    smem = pl.BlockSpec(memory_space=pltpu.SMEM)
    vmem = pl.BlockSpec(memory_space=pltpu.VMEM)
    hbm = pl.BlockSpec(memory_space=pl.ANY)
    return pl.pallas_call(
        functools.partial(kernel, n_src, n_tgt),
        out_shape=jax.ShapeDtypeStruct((dim, share), f32),
        in_specs=[smem, smem, hbm, vmem, vmem, hbm],
        out_specs=vmem,
        scratch_shapes=[
            pltpu.VMEM((cap, edge, edge), bf16),
            pltpu.VMEM((cap, edge, edge), f32),
            pltpu.VMEM((2, edge, LANES), f32),
            pltpu.VMEM((tgt_tiles, tall, edge), bf16),
            pltpu.VMEM((cap, tall, edge), f32),
            pltpu.VMEM((edge, LANES), f32),
            pltpu.VMEM((PAD, edge), f32),
            pltpu.VMEM((LANES, edge), f32),
            pltpu.VMEM((src_tiles, edge, LANES), f32),
            pltpu.VMEM((cap, 8, edge), f32),
            pltpu.VMEM((cap, 8, edge), f32),
            pltpu.VMEM((cap, 8, edge), f32),
            pltpu.VMEM((tgt_tiles, 8, edge), f32),
            pltpu.VMEM((src_tiles, edge), f32),
            pltpu.VMEM((tgt_tiles, edge), f32),
            pltpu.VMEM((n_tgt, src_tiles, edge), f32),
            pltpu.VMEM((n_tgt, src_tiles, edge), f32),
            pltpu.VMEM((n_src, tgt_tiles, edge), f32),
            pltpu.VMEM((n_src, tgt_tiles, edge), f32),
            pltpu.VMEM((n_tgt, tall, share), f32),
            pltpu.VMEM((n_tgt // 2, tall, share), f32),
            pltpu.VMEM((n_tgt // 2 - 1, dim, share), bf16),
            pltpu.VMEM((n_tgt // 2 - 1, dim, share), bf16),
            pltpu.VMEM((n_tgt // 2 - 1, 1, share), f32),
            pltpu.VMEM((n_tgt // 2 - 1, 1, share), f32),
            dma((cap,)),
            dma((tgt_tiles,)),
            dma((n_tgt - 1,)),
            dma((n_tgt - 1,)),
            dma((n_tgt - 1,)),
            dma((n_tgt - 1,)),
            dma((n_src - 1,)),
            dma((n_src - 1,)),
            dma((n_src - 1,)),
            dma((n_src - 1,)),
            dma((n_tgt // 2,)),
            dma((n_tgt // 2,)),
            dma((2, n_tgt // 2 - 1)),
            dma((2, n_tgt // 2 - 1)),
        ],
        compiler_params=pltpu.CompilerParams(
            collective_id=0, has_side_effects=True, vmem_limit_bytes=56 * 1024 * 1024
        ),
    )(
        tile_pairs.T,
        tile_counts,
        tile_cost,
        src_mass,
        tgt_mass,
        targets_t,
    )


def solution(mesh):
    return jax.shard_map(
        functools.partial(local, mesh.shape["src"], mesh.shape["tgt"]),
        mesh=mesh,
        in_specs=(
            P(("src", "tgt"), None, None),
            P(("src", "tgt"), None),
            P(("src", "tgt")),
            P("src"),
            P("tgt"),
            P(None, "tgt"),
        ),
        out_specs=P(None, ("src", "tgt")),
        check_vma=False,
    )
```

```python
import functools

import jax
import jax.numpy as jnp
from jax import lax
from jax.experimental import pallas as pl
from jax.experimental.pallas import tpu as pltpu
from jax.sharding import PartitionSpec as P

MESH = pl.DeviceIdType.MESH
inverse_eps = 50.0 * 1.4426950408889634
negative_floor = -1e30
ROWS = 64
LANES = 128
PAD = 16


def logsumexp0(parts):
    top = jnp.max(parts, axis=0)
    return top + jnp.log2(jnp.sum(jnp.exp2(parts - top[None]), axis=0))


def kernel(
    n_src,
    n_tgt,
    pairs_ref,
    count_ref,
    cost_hbm,
    src_mass_flat,
    tgt_mass_flat,
    targets_hbm,
    out_ref,
    cost,
    q,
    low,
    tgts,
    prods,
    slot_cols,
    slot_rows,
    pad_rows,
    row_pot,
    col_stab,
    col_sum,
    col_fac,
    tgt_pot,
    src_mass_ref,
    tgt_mass_ref,
    row_buf1,
    row_buf2,
    col_buf1,
    col_buf2,
    out_part,
    pair_recv,
    out_send,
    out_recv,
    mass_send,
    mass_recv,
    cost_sem,
    tgts_sem,
    row_send1,
    row_recv1,
    row_send2,
    row_recv2,
    col_send1,
    col_recv1,
    col_send2,
    col_recv2,
    pair_send_sem,
    pair_recv_sem,
    out_send_sem,
    out_recv_sem,
):
    cap, edge = cost.shape[0], cost.shape[1]
    src_tiles, tgt_tiles = src_mass_ref.shape[0], tgt_mass_ref.shape[0]
    dim = targets_hbm.shape[0]
    my_src, my_tgt = lax.axis_index("src"), lax.axis_index("tgt")
    chunks = edge // ROWS

    for k in range(cap):
        pltpu.make_async_copy(cost_hbm.at[k], cost.at[k], cost_sem.at[k]).start()
    for t in range(tgt_tiles):
        pltpu.make_async_copy(
            targets_hbm.at[:, pl.ds(t * edge, edge)], tgts.at[t, pl.ds(0, dim)], tgts_sem.at[t]
        ).start()

    barrier = pltpu.get_barrier_semaphore()
    for off in range(1, n_tgt):
        pl.semaphore_signal(
            barrier, inc=1, device_id={"tgt": lax.rem(my_tgt + off, n_tgt)}, device_id_type=MESH
        )
    for off in range(1, n_src):
        pl.semaphore_signal(
            barrier, inc=1, device_id={"src": lax.rem(my_src + off, n_src)}, device_id_type=MESH
        )

    pad_rows[...] = jnp.zeros_like(pad_rows)
    slot_cols[...] = jnp.zeros_like(slot_cols)
    tgts[:, dim:, :] = jnp.ones((tgt_tiles, PAD, edge), jnp.bfloat16)

    for s in range(src_tiles):
        src_mass_ref[s : s + 1, :] = src_mass_flat[s * edge : (s + 1) * edge].reshape(1, edge)
    for t in range(tgt_tiles):
        tgt_mass_ref[t : t + 1, :] = tgt_mass_flat[t * edge : (t + 1) * edge].reshape(1, edge)

    count = count_ref[0]
    src_of = [lax.rem(pairs_ref[0, k], src_tiles) for k in range(cap)]
    tgt_of = [lax.rem(pairs_ref[1, k], tgt_tiles) for k in range(cap)]
    src_id = [jnp.where(k < count, src_of[k], -1) for k in range(cap)]
    tgt_id = [jnp.where(k < count, tgt_of[k], -1) for k in range(cap)]
    src_rows = lax.broadcasted_iota(jnp.int32, (src_tiles, edge), 0)
    tgt_rows = lax.broadcasted_iota(jnp.int32, (tgt_tiles, edge), 0)
    lane = lax.broadcasted_iota(jnp.int32, (ROWS, LANES), 1)

    def wide(block):
        return jnp.concatenate([block] * (edge // LANES), axis=1)

    def put_column(k, c, value):
        rows = slice(c * ROWS, (c + 1) * ROWS)
        slot_cols[rows, :] = jnp.where(lane == k, value, slot_cols[rows, :])

    def slots_as_rows():
        slot_rows[...] = slot_cols[...].T[:PAD]

    def spread_rows(values):
        pad_rows[0:src_tiles, :] = values
        columns = pad_rows[...].T
        for s in range(src_tiles):
            row_pot[s] = jnp.broadcast_to(columns[:, s : s + 1], (edge, LANES))

    def exchange(buf, axis, me, n, send_sem, recv_sem):
        copies = []
        for off in range(1, n):
            copy = pltpu.make_async_remote_copy(
                src_ref=buf.at[0],
                dst_ref=buf.at[off],
                send_sem=send_sem.at[off - 1],
                recv_sem=recv_sem.at[off - 1],
                device_id={axis: lax.rem(me + off, n)},
                device_id_type=MESH,
            )
            copy.start()
            copies.append(copy)
        for copy in copies:
            copy.wait()

    def merge_logs(parts, ids, rows):
        top = jnp.full(rows.shape, negative_floor, jnp.float32)
        for part, tile in zip(parts, ids):
            top = jnp.maximum(top, jnp.where(rows == tile, part, negative_floor))
        total = jnp.zeros(rows.shape, jnp.float32)
        for part, tile in zip(parts, ids):
            total = total + jnp.where(rows == tile, jnp.exp2(part - top), 0.0)
        return jnp.where(total > 0.0, top + jnp.log2(total), negative_floor)

    def merge_sums(parts, ids, rows):
        total = jnp.zeros(rows.shape, jnp.float32)
        for part, tile in zip(parts, ids):
            total = total + jnp.where(rows == tile, part, 0.0)
        return total

    def halves(combine, block):
        parts = [block[:, at : at + LANES] for at in range(0, edge, LANES)]
        return functools.reduce(combine, parts)

    def in_pairs(step):
        def both(i, carry):
            step(2 * i)
            step(2 * i + 1)
            return carry

        lax.fori_loop(0, cap // 2, both, 0)

    def row_first(i, carry):
        for u in range(2):
            k = 2 * i + u
            pltpu.make_async_copy(cost_hbm.at[k], cost.at[k], cost_sem.at[k]).wait()
            for c in range(chunks):
                rows = slice(c * ROWS, (c + 1) * ROWS)
                tile = cost[k, rows, :].astype(jnp.float32) * inverse_eps
                q[k, rows, :] = tile
                least = jnp.min(halves(jnp.minimum, tile), axis=1, keepdims=True)
                low[u, rows, :] = jnp.broadcast_to(least, (ROWS, LANES))
        for u in range(2):
            k = 2 * i + u
            for c in range(chunks):
                rows = slice(c * ROWS, (c + 1) * ROWS)
                value = jnp.exp2(wide(low[u, rows, :]) - q[k, rows, :])
                total = jnp.sum(halves(jnp.add, value), axis=1, keepdims=True)
                put_column(k, c, jnp.log2(total) - low[u, rows, :])
        return carry

    lax.fori_loop(0, cap // 2, row_first, 0)
    slots_as_rows()
    row_buf1[0] = merge_logs([slot_rows[k : k + 1, :] for k in range(cap)], src_id, src_rows)
    pl.semaphore_wait(barrier, n_tgt - 1 + n_src - 1)
    exchange(row_buf1, "tgt", my_tgt, n_tgt, row_send1, row_recv1)
    spread_rows(jnp.log2(src_mass_ref[...]) - logsumexp0(row_buf1[...]))

    def col_first(i, carry):
        tops = []
        for u in range(2):
            k = 2 * i + u
            s = lax.rem(pairs_ref[0, k], src_tiles)
            top = jnp.full((16, edge), negative_floor, jnp.bfloat16)
            for c in range(chunks):
                rows = slice(c * ROWS, (c + 1) * ROWS)
                rough = (row_pot[s, rows, :] * (1.0 / inverse_eps)).astype(jnp.bfloat16)
                rough = (wide(rough) - cost[k, rows, :]).reshape(ROWS // 16, 16, edge)
                for r in range(ROWS // 16):
                    top = jnp.maximum(top, rough[r])
            top = top.astype(jnp.float32) * inverse_eps
            tops.append(jnp.broadcast_to(jnp.max(top, axis=0, keepdims=True), (8, edge)))
        for u in range(2):
            k = 2 * i + u
            s = lax.rem(pairs_ref[0, k], src_tiles)
            total = jnp.zeros((8, edge), jnp.float32)
            for c in range(chunks):
                rows = slice(c * ROWS, (c + 1) * ROWS)
                score = (wide(row_pot[s, rows, :]) - q[k, rows, :]).reshape(ROWS // 8, 8, edge)
                value = jnp.exp2(score - tops[u][None])
                q[k, rows, :] = value.reshape(ROWS, edge)
                total = total + jnp.sum(value, axis=0)
            col_stab[k] = tops[u]
            col_sum[k] = jnp.broadcast_to(jnp.sum(total, axis=0, keepdims=True), (8, edge))
        return carry

    lax.fori_loop(0, cap // 2, col_first, 0)
    col_buf1[0] = merge_logs(
        [col_stab[k, 0:1, :] + jnp.log2(col_sum[k, 0:1, :]) for k in range(cap)], tgt_id, tgt_rows
    )
    exchange(col_buf1, "src", my_src, n_src, col_send1, col_recv1)
    potential = jnp.log2(tgt_mass_ref[...]) - logsumexp0(col_buf1[...])
    for t in range(tgt_tiles):
        tgt_pot[t] = jnp.broadcast_to(potential[t : t + 1, :], (8, edge))

    def row_second(k):
        t = lax.rem(pairs_ref[1, k], tgt_tiles)
        alive = jnp.full((8, edge), k, jnp.int32) < count
        factor = jnp.where(alive, jnp.exp2(tgt_pot[t] + col_stab[k]), 0.0)
        col_fac[k] = factor
        for c in range(chunks):
            rows = slice(c * ROWS, (c + 1) * ROWS)
            value = q[k, rows, :].reshape(ROWS // 8, 8, edge) * factor[None]
            total = halves(jnp.add, value.reshape(ROWS, edge))
            put_column(k, c, jnp.sum(total, axis=1, keepdims=True))

    in_pairs(row_second)
    slots_as_rows()
    row_buf2[0] = merge_sums([slot_rows[k : k + 1, :] for k in range(cap)], src_id, src_rows)
    exchange(row_buf2, "tgt", my_tgt, n_tgt, row_send2, row_recv2)
    spread_rows(src_mass_ref[...] / jnp.sum(row_buf2[...], axis=0))

    def col_second(k):
        s = lax.rem(pairs_ref[0, k], src_tiles)
        total = jnp.zeros((8, edge), jnp.float32)
        for c in range(chunks):
            rows = slice(c * ROWS, (c + 1) * ROWS)
            value = q[k, rows, :] * wide(row_pot[s, rows, :])
            q[k, rows, :] = value
            total = total + jnp.sum(value.reshape(ROWS // 8, 8, edge), axis=0)
        col_sum[k] = jnp.broadcast_to(jnp.sum(total, axis=0, keepdims=True), (8, edge)) * col_fac[k]

    in_pairs(col_second)
    col_buf2[0] = merge_sums([col_sum[k, 0:1, :] for k in range(cap)], tgt_id, tgt_rows)
    exchange(col_buf2, "src", my_src, n_src, col_send2, col_recv2)
    potential = tgt_mass_ref[...] / jnp.sum(col_buf2[...], axis=0)
    for t in range(tgt_tiles):
        tgt_pot[t] = jnp.broadcast_to(potential[t : t + 1, :], (8, edge))

    for t in range(tgt_tiles):
        pltpu.make_async_copy(
            targets_hbm.at[:, pl.ds(t * edge, edge)], tgts.at[t, pl.ds(0, dim)], tgts_sem.at[t]
        ).wait()

    def map_slot(k):
        t = lax.rem(pairs_ref[1, k], tgt_tiles)
        factor = tgt_pot[t] * col_fac[k]
        left = tgts[t]
        for h in range(edge // 256):
            parts = []
            for c in range(256 // ROWS):
                rows = slice(h * 256 + c * ROWS, h * 256 + (c + 1) * ROWS)
                value = q[k, rows, :].reshape(ROWS // 8, 8, edge)
                parts.append((value * factor[None]).reshape(ROWS, edge).astype(jnp.bfloat16))
            prods[k, :, h * 256 : (h + 1) * 256] = lax.dot_general(
                left,
                jnp.concatenate(parts, axis=0),
                (((1,), (1,)), ((), ())),
                preferred_element_type=jnp.float32,
            )

    in_pairs(map_slot)

    share = out_ref.shape[1]
    tall = dim + PAD
    core, layer, layers = lax.rem(my_tgt, 2), my_tgt // 2, n_tgt // 2

    def pair_copy(j):
        return pltpu.make_async_remote_copy(
            src_ref=out_part.at[2 * j + 1 - core],
            dst_ref=pair_recv.at[j],
            send_sem=pair_send_sem.at[j],
            recv_sem=pair_recv_sem.at[j],
            device_id={"tgt": my_tgt + 1 - 2 * core},
            device_id_type=MESH,
        )

    def layer_copies(other, slot):
        return [
            pltpu.make_async_remote_copy(
                src_ref=sent.at[slot],
                dst_ref=landed.at[slot],
                send_sem=out_send_sem.at[kind, slot],
                recv_sem=out_recv_sem.at[kind, slot],
                device_id={"tgt": 2 * other + core},
                device_id_type=MESH,
            )
            for kind, (sent, landed) in enumerate(((out_send, out_recv), (mass_send, mass_recv)))
        ]

    def ship(j):
        @pl.when(layer != j)
        def _():
            slot = lax.rem(j - layer + layers, layers) - 1
            block = 2 * j + core
            pair_copy(j).wait_recv()
            out_send[slot] = (out_part[block, :dim] + pair_recv[j, :dim]).astype(jnp.bfloat16)
            mass_send[slot] = out_part[block, dim : dim + 1] + pair_recv[j, dim : dim + 1]
            for copy in layer_copies(j, slot):
                copy.start()

    picks = [
        [jnp.where(src_id[k] == s, 1.0, 0.0) for k in range(cap)] for s in range(src_tiles)
    ]
    for place in range(0, src_tiles * edge, LANES):
        s, start = place // edge, place % edge
        total = jnp.zeros((tall, LANES), jnp.float32)
        for k in range(cap):
            total = total + prods[k, :, start : start + LANES] * picks[s][k]
        block, start = place // share, place % share
        out_part[block, :, start : start + LANES] = total
        if (place + LANES) % (2 * share) == 0:
            pair_copy(block // 2).start()
            if block > 2:
                ship(block // 2 - 1)
    ship(layers - 1)

    for off in range(1, layers):
        pair_copy(lax.rem(layer + off, layers)).wait_send()
    pair_copy(layer).wait()
    block = 2 * layer + core
    total = out_part[block, :dim] + pair_recv[layer, :dim]
    mass = out_part[block, dim : dim + 1] + pair_recv[layer, dim : dim + 1]
    for off in range(layers - 1):
        for copy in layer_copies(lax.rem(layer + off + 1, layers), off):
            copy.wait()
        total = total + out_recv[off].astype(jnp.float32)
        mass = mass + mass_recv[off]
    out_ref[...] = total / mass


def local(n_src, n_tgt, tile_cost, tile_pairs, tile_counts, src_mass, tgt_mass, targets_t):
    cap, edge = tile_cost.shape[0], tile_cost.shape[1]
    src_tiles, tgt_tiles = src_mass.shape[0] // edge, tgt_mass.shape[0] // edge
    dim = targets_t.shape[0]
    share = src_mass.shape[0] // n_tgt
    tall = dim + PAD
    f32, bf16 = jnp.float32, jnp.bfloat16
    dma = pltpu.SemaphoreType.DMA
    smem = pl.BlockSpec(memory_space=pltpu.SMEM)
    vmem = pl.BlockSpec(memory_space=pltpu.VMEM)
    hbm = pl.BlockSpec(memory_space=pl.ANY)
    return pl.pallas_call(
        functools.partial(kernel, n_src, n_tgt),
        out_shape=jax.ShapeDtypeStruct((dim, share), f32),
        in_specs=[smem, smem, hbm, vmem, vmem, hbm],
        out_specs=vmem,
        scratch_shapes=[
            pltpu.VMEM((cap, edge, edge), bf16),
            pltpu.VMEM((cap, edge, edge), f32),
            pltpu.VMEM((2, edge, LANES), f32),
            pltpu.VMEM((tgt_tiles, tall, edge), bf16),
            pltpu.VMEM((cap, tall, edge), f32),
            pltpu.VMEM((edge, LANES), f32),
            pltpu.VMEM((PAD, edge), f32),
            pltpu.VMEM((LANES, edge), f32),
            pltpu.VMEM((src_tiles, edge, LANES), f32),
            pltpu.VMEM((cap, 8, edge), f32),
            pltpu.VMEM((cap, 8, edge), f32),
            pltpu.VMEM((cap, 8, edge), f32),
            pltpu.VMEM((tgt_tiles, 8, edge), f32),
            pltpu.VMEM((src_tiles, edge), f32),
            pltpu.VMEM((tgt_tiles, edge), f32),
            pltpu.VMEM((n_tgt, src_tiles, edge), f32),
            pltpu.VMEM((n_tgt, src_tiles, edge), f32),
            pltpu.VMEM((n_src, tgt_tiles, edge), f32),
            pltpu.VMEM((n_src, tgt_tiles, edge), f32),
            pltpu.VMEM((n_tgt, tall, share), f32),
            pltpu.VMEM((n_tgt // 2, tall, share), f32),
            pltpu.VMEM((n_tgt // 2 - 1, dim, share), bf16),
            pltpu.VMEM((n_tgt // 2 - 1, dim, share), bf16),
            pltpu.VMEM((n_tgt // 2 - 1, 1, share), f32),
            pltpu.VMEM((n_tgt // 2 - 1, 1, share), f32),
            dma((cap,)),
            dma((tgt_tiles,)),
            dma((n_tgt - 1,)),
            dma((n_tgt - 1,)),
            dma((n_tgt - 1,)),
            dma((n_tgt - 1,)),
            dma((n_src - 1,)),
            dma((n_src - 1,)),
            dma((n_src - 1,)),
            dma((n_src - 1,)),
            dma((n_tgt // 2,)),
            dma((n_tgt // 2,)),
            dma((2, n_tgt // 2 - 1)),
            dma((2, n_tgt // 2 - 1)),
        ],
        compiler_params=pltpu.CompilerParams(
            collective_id=0, has_side_effects=True, vmem_limit_bytes=56 * 1024 * 1024
        ),
    )(
        tile_pairs.T,
        tile_counts,
        tile_cost,
        src_mass,
        tgt_mass,
        targets_t,
    )


def solution(mesh):
    return jax.shard_map(
        functools.partial(local, mesh.shape["src"], mesh.shape["tgt"]),
        mesh=mesh,
        in_specs=(
            P(("src", "tgt"), None, None),
            P(("src", "tgt"), None),
            P(("src", "tgt")),
            P("src"),
            P("tgt"),
            P(None, "tgt"),
        ),
        out_specs=P(None, ("src", "tgt")),
        check_vma=False,
    )
```
